32 devices in a mesh: grp: 2 (over x), row: 8 (over z, y), col: 2 (over core).
Axes of the slice: x: 2, y: 2, z: 4, core: 2. Of those that a mesh axis runs over, the one named last changes fastest.
Arguments:
- query_window: bfloat16 [16, 8, 128, 1280], P(('grp', 'row'), 'col'), parts along dimension 0, may hold values from -80 to 80
- key_window: bfloat16 [16, 8, 128, 1280], P(('grp', 'row'), 'col'), parts along dimension 0, may hold values from -9 to 9
- value_window: bfloat16 [16, 8, 128, 1280], P(('grp', 'row'), 'col'), parts along dimension 0, may hold values from -6 to 6
- query_index: bfloat16 [16, 8, 128, 1280], P(('grp', 'row'), 'col'), parts along dimension 0, may hold values from -80 to 80
- key_index: bfloat16 [16, 8, 128, 1280], P(('grp', 'row'), 'col'), parts along dimension 0, may hold values from -9 to 9
- proj_weight: bfloat16 [1280, 1024], replicated, may hold values from -0.5 to 0.5
- proj_bias: float32 [1024], replicated, may hold values from -3 to 3
- first_kernel: bfloat16 [3, 3, 256, 256], replicated, may hold values from -0.125 to 0.125
- first_bias: float32 [256], replicated, may hold values from -3 to 3
- second_kernel: bfloat16 [3, 3, 256, 256], replicated, may hold values from -0.125 to 0.125
- second_bias: float32 [256], replicated, may hold values from -3 to 3
Outputs:
- fine_field: bfloat16 [256, 256, 256], P(('grp', 'row'), 'col'), parts along dimension 0
The draws below stay inside these ranges and needn't reach their ends.
There are 2 independent parts, one for each index of `grp`. The reference program is written for one: setup_inputs(seed, part) draws one part's arguments, and reference() takes and returns one part's arrays. A program takes and returns all parts, laid end to end along the dimension named above; an argument that names none is the same for every part. Nothing has to cross between parts.
All inputs are finite; a program needn't handle non-finite values.
Results may differ from the reference program's by a relative error of at most 0.0048.
Values may be sent and summed in bfloat16 or wider, within the bound.
No kernel may reach another device: no remote copies, remote signals or barrier semaphores. Data moves between devices by JAX's collectives and lax.ppermute only.
A program may use at most 64 MiB of HBM per device.

```python
import math
import jax
import jax.numpy as jnp
from jax import lax

HEADS = 8
HEAD_DIM = 160
CHANNELS = 256
TILE_ROWS = 8
TILE_COLS = 16
INNER = 1280
WIN_TOKENS = 128
WIN_ROWS = 8
WIN_COLS = 8


def paired_draw(key):
    layout = (WIN_ROWS * WIN_COLS, WIN_TOKENS, HEADS, HEAD_DIM)
    key_draw = 1.41 * jax.random.truncated_normal(jax.random.fold_in(key, 11), -6.0, 6.0, layout, jnp.float32)
    query_draw = 1.41 * jax.random.truncated_normal(jax.random.fold_in(key, 12), -6.0, 6.0, layout, jnp.float32)
    final = (WIN_ROWS, WIN_COLS, WIN_TOKENS, HEADS * HEAD_DIM)
    return (query_draw.reshape(final).astype(jnp.bfloat16), key_draw.reshape(final).astype(jnp.bfloat16))


def draw_query_window(key, part):
    return paired_draw(jax.random.fold_in(key, 101))[0]


def draw_key_window(key, part):
    return paired_draw(jax.random.fold_in(key, 101))[1]


def draw_query_index(key, part):
    return paired_draw(jax.random.fold_in(key, 202))[0]


def draw_key_index(key, part):
    return paired_draw(jax.random.fold_in(key, 202))[1]


def steps_of(stream_key, dims, pieces, low, top_value):
    loudness = 1.0
    for position, parts in pieces:
        heights = jax.random.uniform(jax.random.fold_in(jax.random.fold_in(stream_key, 6), position), (parts,), jnp.float32, low / len(pieces), top_value / len(pieces))
        loudness = loudness * jnp.repeat(jnp.exp(heights), dims[position] // parts).reshape((-1,) + (1,) * (len(dims) - 1 - position))
    return loudness


def scatter_about(stream_key, extent, spread, reach, cuts=(), held_as=jnp.bfloat16):
    drawn = spread * jax.random.normal(stream_key, extent, jnp.float32)
    if cuts:
        drawn = drawn * steps_of(stream_key, extent, cuts, -0.22, 0.18)
    return jnp.clip(drawn, -reach, reach).astype(held_as)


def setup_inputs(seed: int = 0, part: int = 0) -> dict:
    keys = jax.random.split(jax.random.key(seed), 12)
    part_keys = jax.random.split(jax.random.fold_in(keys[11], part), 12)
    return {
        "query_window": draw_query_window(jax.random.fold_in(jax.random.fold_in(keys[11], part), 71), part),
        "key_window": draw_key_window(jax.random.fold_in(jax.random.fold_in(keys[11], part), 71), part),
        "value_window": scatter_about(part_keys[2], (WIN_ROWS, WIN_COLS, WIN_TOKENS, INNER), 1.0, 6.0, ((0, 8), (1, 2))),
        "query_index": draw_query_index(jax.random.fold_in(jax.random.fold_in(keys[11], part), 71), part),
        "key_index": draw_key_index(jax.random.fold_in(jax.random.fold_in(keys[11], part), 71), part),
        "proj_weight": scatter_about(keys[5], (INNER, 4 * CHANNELS), (INNER // 8) ** -0.5, 0.5),
        "proj_bias": scatter_about(keys[6], (4 * CHANNELS,), 0.5, 3.0, (), jnp.float32),
        "first_kernel": scatter_about(keys[7], (3, 3, CHANNELS, CHANNELS), (9 * CHANNELS) ** -0.5, 0.125),
        "first_bias": scatter_about(keys[8], (CHANNELS,), 0.5, 3.0, (), jnp.float32),
        "second_kernel": scatter_about(keys[9], (3, 3, CHANNELS, CHANNELS), (9 * CHANNELS) ** -0.5, 0.125),
        "second_bias": scatter_about(keys[10], (CHANNELS,), 0.5, 3.0, (), jnp.float32),
    }


def attend(queries, key_rows, values):
    scores = jnp.einsum('blhd,bmhd->bhlm', queries.astype(jnp.float32), key_rows.astype(jnp.float32)) / math.sqrt(HEAD_DIM)
    highest = lax.optimization_barrier(jnp.max(scores, axis=-1, keepdims=True))
    raised = jnp.exp(scores - highest)
    weights = (raised / lax.optimization_barrier(jnp.sum(raised, axis=-1, keepdims=True))).astype(jnp.bfloat16)
    mixed = jnp.einsum('bhlm,bmhd->blhd', weights.astype(jnp.float32), values.astype(jnp.float32))
    return mixed.astype(jnp.bfloat16)

def convolve(image, kernel, bias):
    height, breadth, depth = image.shape
    padded = jnp.pad(image, ((1, 1), (1, 1), (0, 0)))
    total = jnp.zeros((height * breadth, kernel.shape[-1]), jnp.float32)
    for row_shift in range(3):
        for col_shift in range(3):
            cells = padded[row_shift:row_shift + height, col_shift:col_shift + breadth].reshape(-1, depth)
            total = total + jnp.dot(cells, kernel[row_shift, col_shift], preferred_element_type=jnp.float32)
    return (total + bias).reshape(height, breadth, -1)

def reference(query_window, key_window, value_window, query_index, key_index, proj_weight, proj_bias, first_kernel, first_bias, second_kernel, second_bias):
    layout = (WIN_ROWS * WIN_COLS, WIN_TOKENS, HEADS, HEAD_DIM)
    window_out = attend(query_window.reshape(layout), key_window.reshape(layout), value_window.reshape(layout))
    index_out = attend(jnp.swapaxes(query_index.reshape(layout), 0, 1), jnp.swapaxes(key_index.reshape(layout), 0, 1), jnp.swapaxes(window_out, 0, 1))
    index_rows = jnp.swapaxes(index_out, 0, 1).reshape(-1, HEADS * HEAD_DIM)
    projected = (jnp.dot(index_rows, proj_weight, preferred_element_type=jnp.float32) + proj_bias).astype(jnp.bfloat16)
    grouped = projected.reshape(WIN_ROWS, WIN_COLS, TILE_ROWS, TILE_COLS, 2, 2, CHANNELS)
    shuffled = jnp.transpose(grouped, (0, 2, 4, 1, 3, 5, 6)).reshape(WIN_ROWS * TILE_ROWS * 2, WIN_COLS * TILE_COLS * 2, CHANNELS)
    activated = jax.nn.gelu(convolve(shuffled, first_kernel, first_bias)).astype(jnp.bfloat16)
    return convolve(activated, second_kernel, second_bias).astype(jnp.bfloat16)
```

```python
import functools
import math

import jax
import jax.numpy as jnp
from jax import lax
from jax.experimental import pallas as pl
from jax.experimental.pallas import tpu as pltpu
from jax.sharding import PartitionSpec as P

HEADS = 8
HEAD_DIM = 160
CHANNELS = 256
TILE_ROWS = 8
TILE_COLS = 16
LANES = 128
EDGE = 16
SPAN = 2 * LANES
VMEM_BYTES = 40 * 1024 * 1024


def params(steps=0):
    return pltpu.CompilerParams(
        dimension_semantics=("arbitrary",) * steps if steps else None,
        vmem_limit_bytes=VMEM_BYTES,
    )


def head_start(head):
    return head * HEAD_DIM // LANES * LANES


def head_mask(head):
    lane = lax.broadcasted_iota(jnp.int32, (1, SPAN), 1) + head_start(head)
    return (lane >= head * HEAD_DIM) & (lane < (head + 1) * HEAD_DIM)


def joined_heads(mixed):
    tiles = []
    lane = lax.broadcasted_iota(jnp.int32, (1, LANES), 1)
    for tile in range(HEADS * HEAD_DIM // LANES):
        base = tile * LANES
        first, last = base // HEAD_DIM, (base + LANES - 1) // HEAD_DIM
        pieces = []
        for head in (first, last):
            at = base - head_start(head)
            pieces.append(mixed[head][:, at : at + LANES])
        if first == last:
            tiles.append(pieces[0])
        else:
            tiles.append(jnp.where(lane < last * HEAD_DIM - base, pieces[0], pieces[1]))
    return jnp.concatenate(tiles, axis=1)


def softmax_rows(scores):
    raised = jnp.exp(scores - jnp.max(scores, axis=-1, keepdims=True))
    return (raised / jnp.sum(raised, axis=-1, keepdims=True)).astype(jnp.bfloat16)


def window_kernel(query, key_rows, value, out):
    mixed = []
    for head in range(HEADS):
        lanes = pl.ds(head_start(head), SPAN)
        masked = jnp.where(head_mask(head), query[0, :, lanes], 0)
        scores = lax.dot_general(
            masked, key_rows[0, :, lanes], (((1,), (1,)), ((), ())),
            preferred_element_type=jnp.float32,
        ) * (1.0 / math.sqrt(HEAD_DIM))
        mixed.append(
            jnp.dot(softmax_rows(scores), value[0, :, lanes], preferred_element_type=jnp.float32)
        )
    out[0] = joined_heads(mixed).astype(jnp.bfloat16)


def window_attend(query, key_rows, value):
    windows, tokens, features = query.shape
    block = pl.BlockSpec((1, tokens, features), lambda w: (w, 0, 0))
    return pl.pallas_call(
        window_kernel,
        grid=(windows,),
        in_specs=[block] * 3,
        out_specs=block,
        out_shape=jax.ShapeDtypeStruct(query.shape, jnp.bfloat16),
        compiler_params=params(1),
    )(query, key_rows, value)


def weights_kernel(tokens, query, key_rows, out):
    rows = query.shape[0]
    head = pl.program_id(0)
    start = head * HEAD_DIM // LANES * LANES
    lanes = pl.ds(pl.multiple_of(start, LANES), SPAN)
    lane = lax.broadcasted_iota(jnp.int32, (1, SPAN), 1) + start
    inside = (lane >= head * HEAD_DIM) & (lane < (head + 1) * HEAD_DIM)
    masked = jnp.where(inside, query[:, lanes], 0)
    scores = lax.dot_general(
        masked, key_rows[:, lanes], (((1,), (1,)), ((), ())),
        preferred_element_type=jnp.float32,
    ) * (1.0 / math.sqrt(HEAD_DIM))
    token_row = lax.broadcasted_iota(jnp.int32, (rows, 1), 0) % tokens
    token_col = lax.broadcasted_iota(jnp.int32, (1, rows), 1) % tokens
    out[0] = softmax_rows(jnp.where(token_row == token_col, scores, -jnp.inf))


def index_weights(query, key_rows, tokens):
    rows, features = query.shape
    whole = pl.BlockSpec((rows, features), lambda h: (0, 0))
    return pl.pallas_call(
        functools.partial(weights_kernel, tokens),
        grid=(HEADS,),
        in_specs=[whole] * 2,
        out_specs=pl.BlockSpec((1, rows, rows), lambda h: (h, 0, 0)),
        out_shape=jax.ShapeDtypeStruct((HEADS, rows, rows), jnp.bfloat16),
        compiler_params=params(1),
    )(query, key_rows)


def project_kernel(weights, value, proj_weight, proj_bias, out):
    mixed = []
    for head in range(HEADS):
        lanes = pl.ds(head_start(head), SPAN)
        mixed.append(
            jnp.dot(weights[head], value[:, lanes], preferred_element_type=jnp.float32)
        )
    joined = joined_heads(mixed).astype(jnp.bfloat16)
    total = jnp.dot(joined, proj_weight[...], preferred_element_type=jnp.float32)
    out[...] = (total + proj_bias[...]).astype(jnp.bfloat16)


def project(weights, value, proj_weight, proj_bias):
    rows, features = value.shape
    width = proj_weight.shape[1]
    block = rows // 2
    return pl.pallas_call(
        project_kernel,
        grid=(rows // block,),
        in_specs=[
            pl.BlockSpec((HEADS, block, rows), lambda r: (0, r, 0)),
            pl.BlockSpec((rows, features), lambda r: (0, 0)),
            pl.BlockSpec((features, width), lambda r: (0, 0)),
            pl.BlockSpec((1, width), lambda r: (0, 0)),
        ],
        out_specs=pl.BlockSpec((block, width), lambda r: (r, 0)),
        out_shape=jax.ShapeDtypeStruct((rows, width), jnp.bfloat16),
        compiler_params=params(1),
    )(weights, value, proj_weight, proj_bias.reshape(1, width))


def conv_kernel(
    rows, cols, image, above, below, left, right, keep,
    first_kernel, first_bias, second_kernel, second_bias, out,
    taken, even, odd, acted, woven,
):
    pitch = cols + EDGE
    depth = CHANNELS
    place = lax.broadcasted_iota(jnp.int32, (EDGE, 1), 0)
    half = 2 * depth

    def gap_of(row):
        block = jnp.zeros((EDGE, half), jnp.float32)
        if row >= 1:
            token, sub = (row - 1) // 2, (row - 1) % 2
            block = jnp.where(
                place == 0,
                right[token : token + 1, sub * half : (sub + 1) * half].astype(jnp.float32),
                block,
            )
        if row < 2 * (rows + 2):
            token, sub = row // 2, row % 2
            block = jnp.where(
                place == EDGE - 1,
                left[token : token + 1, sub * half : (sub + 1) * half].astype(jnp.float32),
                block,
            )
        return block

    taken[0:EDGE, 0:depth] = jnp.zeros((EDGE, depth), jnp.bfloat16)
    for i in range(rows + 2):
        if i == 0:
            body = above[...]
        elif i == rows + 1:
            body = below[...]
        else:
            body = image[pl.ds((i - 1) * cols, cols), :]
        body = body.astype(jnp.float32)
        for p in range(2):
            lanes = slice(p * half, (p + 1) * half)
            y = 2 * i + p
            line = jnp.concatenate([gap_of(y), body[:, lanes], gap_of(y + 1)], axis=0)
            length = line.shape[0]
            base = y * pitch
            taken[base : base + length, depth : 3 * depth] = line.astype(jnp.bfloat16)
            later = pltpu.roll(line[:, depth:], 1, 0)
            sooner = pltpu.roll(line[:, :depth], length - 1, 0)
            taken[base + EDGE : base + length, 0:depth] = later[EDGE:].astype(jnp.bfloat16)
            taken[base : base + pitch, 3 * depth :] = sooner[:pitch].astype(jnp.bfloat16)
    last = 2 * (rows + 2) * pitch
    taken[last : last + EDGE, 3 * depth :] = jnp.zeros((EDGE, depth), jnp.bfloat16)

    lines = 2 * rows
    total = (lines + 2) * pitch + EDGE
    even[0:EDGE] = jnp.zeros((EDGE, depth), jnp.float32)
    odd[0:EDGE] = jnp.zeros((EDGE, depth), jnp.float32)
    even[EDGE + total :] = jnp.zeros((EDGE, depth), jnp.float32)
    odd[EDGE + total :] = jnp.zeros((EDGE, depth), jnp.float32)

    def taps(source, kernel, at, size, q):
        found = None
        for r in range(3):
            part = jnp.dot(
                source[pl.ds(at + r * pitch, size), q * depth : (q + 3) * depth], kernel[r],
                preferred_element_type=jnp.float32,
            )
            found = part if found is None else found + part
        return found

    pieces = 3
    step = -(-total // pieces // EDGE) * EDGE
    for at in range(0, total, step):
        size = min(step, total - at)
        kept = keep[at : at + size, :] > 0.0
        kept = jnp.concatenate([kept] * (depth // LANES), axis=1)
        for q, held in ((0, even), (1, odd)):
            value = taps(taken, first_kernel, at, size, q) + first_bias[...]
            value = jax.nn.gelu(value)
            held[EDGE + at : EDGE + at + size] = jnp.where(kept, value, 0.0)
    acted[:, depth : 2 * depth] = even[EDGE : EDGE + total].astype(jnp.bfloat16)
    acted[:, 2 * depth : 3 * depth] = odd[EDGE : EDGE + total].astype(jnp.bfloat16)
    acted[:, 0:depth] = odd[EDGE - 1 : EDGE - 1 + total].astype(jnp.bfloat16)
    acted[:, 3 * depth :] = even[EDGE + 1 : EDGE + 1 + total].astype(jnp.bfloat16)

    group = max(lines // 4, 1)
    for at in range(0, lines, group):
        size = group * pitch - EDGE
        for q in range(2):
            value = taps(acted, second_kernel, EDGE + at * pitch, size, q) + second_bias[...]
            for y in range(group):
                for lane in range(depth // LANES):
                    woven[lane, pl.ds((at + y) * 2 * cols + q, cols, stride=2), :] = value[
                        y * pitch : y * pitch + cols, lane * LANES : (lane + 1) * LANES
                    ]
    for lane in range(depth // LANES):
        out[:, lane * LANES : (lane + 1) * LANES] = woven[lane].astype(jnp.bfloat16)


def convolve_twice(image, above, below, left, right, keep, first_kernel, first_bias, second_kernel, second_bias):
    rows, cols, width = image.shape
    pitch = cols + EDGE
    total = (2 * rows + 2) * pitch + EDGE
    depth = CHANNELS
    found = pl.pallas_call(
        functools.partial(conv_kernel, rows, cols),
        out_shape=jax.ShapeDtypeStruct((4 * rows * cols, depth), jnp.bfloat16),
        in_specs=[pl.BlockSpec(memory_space=pltpu.VMEM)] * 10,
        out_specs=pl.BlockSpec(memory_space=pltpu.VMEM),
        scratch_shapes=[
            pltpu.VMEM(((2 * rows + 4) * pitch + EDGE, 4 * depth), jnp.bfloat16),
            pltpu.VMEM((total + 2 * EDGE, depth), jnp.float32),
            pltpu.VMEM((total + 2 * EDGE, depth), jnp.float32),
            pltpu.VMEM((total, 4 * depth), jnp.bfloat16),
            pltpu.VMEM((depth // LANES, 4 * rows * cols, LANES), jnp.float32),
        ],
        compiler_params=params(),
    )(
        image.reshape(rows * cols, width), above, below, left, right, keep,
        first_kernel.reshape(3, 3 * depth, depth), first_bias.reshape(1, depth),
        second_kernel.reshape(3, 3 * depth, depth), second_bias.reshape(1, depth),
    )
    return found.reshape(2 * rows, 2 * cols, depth)


def kept_rows(rows, cols):
    pitch = cols + EDGE
    lines = 2 * rows
    total = (lines + 2) * pitch + EDGE
    row, col = lax.axis_index("row"), lax.axis_index("col")
    top, bottom = row == 0, row == lax.axis_size("row") - 1
    start, end = col == 0, col == lax.axis_size("col") - 1
    flat = jnp.arange(total)
    line, place = flat // pitch - 1, flat % pitch - EDGE
    wrapped = place == -EDGE
    line = jnp.where(wrapped, line - 1, line)
    place = jnp.where(wrapped, cols, place)
    outside = (
        ((line < 0) & top) | ((line >= lines) & bottom)
        | ((place < 0) & start) | ((place >= cols) & end)
    )
    return jnp.broadcast_to(jnp.where(outside, 0.0, 1.0)[:, None], (total, LANES)).astype(jnp.float32)


def shifted(value, axis, by):
    size = lax.axis_size(axis)
    pairs = [(i, i + by) for i in range(size) if 0 <= i + by < size]
    return lax.ppermute(value, axis, pairs)


def shards(
    query_window, key_window, value_window, query_index, key_index,
    proj_weight, proj_bias, first_kernel, first_bias, second_kernel, second_bias,
):
    rows_dev, cols_dev, tokens_win, features = query_window.shape
    windows = rows_dev * cols_dev
    axes = ("row", "col")
    owners = lax.axis_size("row") * lax.axis_size("col")
    owned = tokens_win // owners

    def dealt(value):
        return jnp.swapaxes(value.reshape(windows, owners, owned, features), 0, 1)

    def exchanged(value):
        return lax.all_to_all(value, axes, split_axis=0, concat_axis=0, tiled=True)

    pair = exchanged(jnp.concatenate([dealt(query_index), dealt(key_index)], axis=1))
    flat = (windows, tokens_win, features)
    window_out = window_attend(
        query_window.reshape(flat), key_window.reshape(flat), value_window.reshape(flat)
    )
    keep = kept_rows(rows_dev * TILE_ROWS, cols_dev * TILE_COLS)
    values = exchanged(dealt(window_out)).reshape(-1, features)
    queries = pair[:, :windows].reshape(-1, features)
    key_rows = pair[:, windows:].reshape(-1, features)
    weights = index_weights(queries, key_rows, owned)
    projected = project(weights, values, proj_weight, proj_bias)
    width = projected.shape[-1]
    returned = exchanged(projected.reshape(owners, windows, owned, width))
    tokens = jnp.swapaxes(returned, 0, 1).reshape(rows_dev, cols_dev, TILE_ROWS, TILE_COLS, width)
    image = jnp.transpose(tokens, (0, 2, 1, 3, 4)).reshape(
        rows_dev * TILE_ROWS, cols_dev * TILE_COLS, width
    )
    above = shifted(image[-1:], "row", 1)
    below = shifted(image[:1], "row", -1)
    tall = jnp.concatenate([above[:, -1], image[:, -1], below[:, -1]], axis=0)
    left = shifted(tall, "col", 1)
    tall = jnp.concatenate([above[:, 0], image[:, 0], below[:, 0]], axis=0)
    right = shifted(tall, "col", -1)
    return convolve_twice(
        image, above[0], below[0], left, right, keep,
        first_kernel, first_bias, second_kernel, second_bias,
    )


def solution(mesh):
    spread = P(("grp", "row"), "col", None, None)
    in_specs = (spread,) * 5 + (P(),) * 6
    out_specs = P(("grp", "row"), "col", None)
    return jax.shard_map(shards, mesh=mesh, in_specs=in_specs, out_specs=out_specs, check_vma=False)
```

```python
import functools
import math

import jax
import jax.numpy as jnp
from jax import lax
from jax.experimental import pallas as pl
from jax.experimental.pallas import tpu as pltpu
from jax.sharding import PartitionSpec as P

HEADS = 8
HEAD_DIM = 160
CHANNELS = 256
TILE_ROWS = 8
TILE_COLS = 16
LANES = 128
EDGE = 16
SPAN = 2 * LANES
VMEM_BYTES = 40 * 1024 * 1024


def params(steps=0):
    return pltpu.CompilerParams(
        dimension_semantics=("arbitrary",) * steps if steps else None,
        vmem_limit_bytes=VMEM_BYTES,
    )


def head_start(head):
    return head * HEAD_DIM // LANES * LANES


def head_mask(head):
    lane = lax.broadcasted_iota(jnp.int32, (1, SPAN), 1) + head_start(head)
    return (lane >= head * HEAD_DIM) & (lane < (head + 1) * HEAD_DIM)


def joined_heads(mixed):
    tiles = []
    lane = lax.broadcasted_iota(jnp.int32, (1, LANES), 1)
    for tile in range(len(mixed) * HEAD_DIM // LANES):
        base = tile * LANES
        first, last = base // HEAD_DIM, (base + LANES - 1) // HEAD_DIM
        pieces = []
        for head in (first, last):
            at = base - head_start(head)
            pieces.append(mixed[head][:, at : at + LANES])
        if first == last:
            tiles.append(pieces[0])
        else:
            tiles.append(jnp.where(lane < last * HEAD_DIM - base, pieces[0], pieces[1]))
    return jnp.concatenate(tiles, axis=1)


def softmax_rows(scores):
    raised = jnp.exp(scores - jnp.max(scores, axis=-1, keepdims=True))
    return (raised / jnp.sum(raised, axis=-1, keepdims=True)).astype(jnp.bfloat16)


def window_kernel(query, key_rows, value, out):
    mixed = []
    for head in range(HEADS):
        lanes = pl.ds(head_start(head), SPAN)
        masked = jnp.where(head_mask(head), query[0, :, lanes], 0)
        scores = lax.dot_general(
            masked, key_rows[0, :, lanes], (((1,), (1,)), ((), ())),
            preferred_element_type=jnp.float32,
        ) * (1.0 / math.sqrt(HEAD_DIM))
        mixed.append(
            jnp.dot(softmax_rows(scores), value[0, :, lanes], preferred_element_type=jnp.float32)
        )
    joined = joined_heads(mixed).astype(jnp.bfloat16)
    parts, features = out.shape[0], out.shape[-1]
    for part in range(parts):
        out[part, 0] = joined[:, part * features : (part + 1) * features]


def window_attend(query, key_rows, value, parts):
    windows, tokens, features = query.shape
    result = (parts, windows, tokens, features // parts)
    block = pl.BlockSpec((1, tokens, features), lambda w: (w, 0, 0))
    return pl.pallas_call(
        window_kernel,
        grid=(windows,),
        in_specs=[block] * 3,
        out_specs=pl.BlockSpec((parts, 1, tokens, features // parts), lambda w: (0, w, 0, 0)),
        out_shape=jax.ShapeDtypeStruct(result, jnp.bfloat16),
        compiler_params=params(1),
    )(query, key_rows, value)


def weights_kernel(tokens, query_near, query_far, key_near, key_far, out):
    head = pl.program_id(0)
    start = head * HEAD_DIM // LANES * LANES
    lanes = pl.ds(pl.multiple_of(start, LANES), SPAN)
    lane = lax.broadcasted_iota(jnp.int32, (1, SPAN), 1) + start
    inside = (lane >= head * HEAD_DIM) & (lane < (head + 1) * HEAD_DIM)
    query = jnp.concatenate([query_near[:, lanes], query_far[:, lanes]], axis=0)
    key_rows = jnp.concatenate([key_near[:, lanes], key_far[:, lanes]], axis=0)
    scores = lax.dot_general(
        jnp.where(inside, query, 0), key_rows, (((1,), (1,)), ((), ())),
        preferred_element_type=jnp.float32,
    ) * (1.0 / math.sqrt(HEAD_DIM))
    rows = query.shape[0]
    token_row = lax.broadcasted_iota(jnp.int32, (rows, 1), 0) % tokens
    token_col = lax.broadcasted_iota(jnp.int32, (1, rows), 1) % tokens
    out[0] = softmax_rows(jnp.where(token_row == token_col, scores, -jnp.inf))


def index_weights(query_near, query_far, key_near, key_far, tokens):
    rows, features = query_near.shape
    heads = features // HEAD_DIM
    whole = pl.BlockSpec((rows, features), lambda h: (0, 0))
    return pl.pallas_call(
        functools.partial(weights_kernel, tokens),
        grid=(heads,),
        in_specs=[whole] * 4,
        out_specs=pl.BlockSpec((1, 2 * rows, 2 * rows), lambda h: (h, 0, 0)),
        out_shape=jax.ShapeDtypeStruct((heads, 2 * rows, 2 * rows), jnp.bfloat16),
        compiler_params=params(1),
    )(query_near, query_far, key_near, key_far)


def mix_kernel(weights, *refs):
    pieces, (near, far) = refs[:-2], refs[-2:]
    inner, cores, _, features = pieces[0].shape
    value = jnp.concatenate(
        [piece[j, core] for core in range(cores) for piece in pieces for j in range(inner)], axis=0
    )
    mixed = []
    for head in range(features // HEAD_DIM):
        lanes = slice(head_start(head), head_start(head) + SPAN)
        mixed.append(jnp.dot(weights[head], value[:, lanes], preferred_element_type=jnp.float32))
    joined = joined_heads(mixed).astype(jnp.bfloat16)
    half = value.shape[0] // 2
    near[...] = joined[:half]
    far[...] = joined[half:]


def index_mix(weights, pieces):
    rows, features = weights.shape[1], pieces[0].shape[-1]
    result = jax.ShapeDtypeStruct((rows // 2, features), jnp.bfloat16)
    return pl.pallas_call(
        mix_kernel,
        in_specs=[pl.BlockSpec(memory_space=pltpu.VMEM)] * (1 + len(pieces)),
        out_specs=[pl.BlockSpec(memory_space=pltpu.VMEM)] * 2,
        out_shape=[result, result],
        compiler_params=params(),
    )(weights, *pieces)


def project_kernel(near, far, proj_weight, proj_bias, out):
    joined = jnp.concatenate([near[...], far[...]], axis=1)
    total = jnp.dot(joined, proj_weight[...], preferred_element_type=jnp.float32)
    out[...] = (total + proj_bias[...]).astype(jnp.bfloat16)


def project(near, far, proj_weight, proj_bias):
    return pl.pallas_call(
        project_kernel,
        in_specs=[pl.BlockSpec(memory_space=pltpu.VMEM)] * 4,
        out_specs=pl.BlockSpec(memory_space=pltpu.VMEM),
        out_shape=jax.ShapeDtypeStruct((near.shape[0], proj_weight.shape[1]), jnp.bfloat16),
        compiler_params=params(),
    )(near, far, proj_weight, proj_bias.reshape(1, -1))


def line_of(line, rows):
    quarter = rows // 4
    if line < quarter:
        return 0, line
    if line < 3 * quarter:
        return 1, line - quarter
    return 0, line - 2 * quarter


def conv_kernel(
    rows, cols, outer, middle, above, below, left, right, keep,
    first_kernel, first_bias, second_kernel, second_bias, out,
    taken, even, odd, acted, woven,
):
    pitch = cols + EDGE
    depth = CHANNELS
    place = lax.broadcasted_iota(jnp.int32, (EDGE, 1), 0)
    half = 2 * depth

    def gap_of(row):
        block = jnp.zeros((EDGE, half), jnp.float32)
        if row >= 1:
            token, sub = (row - 1) // 2, (row - 1) % 2
            block = jnp.where(
                place == 0,
                right[token : token + 1, sub * half : (sub + 1) * half].astype(jnp.float32),
                block,
            )
        if row < 2 * (rows + 2):
            token, sub = row // 2, row % 2
            block = jnp.where(
                place == EDGE - 1,
                left[token : token + 1, sub * half : (sub + 1) * half].astype(jnp.float32),
                block,
            )
        return block

    taken[0:EDGE, 0:depth] = jnp.zeros((EDGE, depth), jnp.bfloat16)
    for i in range(rows + 2):
        if i == 0:
            body = above[...]
        elif i == rows + 1:
            body = below[...]
        else:
            part, at = line_of(i - 1, rows)
            body = (outer, middle)[part][pl.ds(at * cols, cols), :]
        body = body.astype(jnp.float32)
        for p in range(2):
            lanes = slice(p * half, (p + 1) * half)
            y = 2 * i + p
            line = jnp.concatenate([gap_of(y), body[:, lanes], gap_of(y + 1)], axis=0)
            length = line.shape[0]
            base = y * pitch
            taken[base : base + length, depth : 3 * depth] = line.astype(jnp.bfloat16)
            later = pltpu.roll(line[:, depth:], 1, 0)
            sooner = pltpu.roll(line[:, :depth], length - 1, 0)
            taken[base + EDGE : base + length, 0:depth] = later[EDGE:].astype(jnp.bfloat16)
            taken[base : base + pitch, 3 * depth :] = sooner[:pitch].astype(jnp.bfloat16)
    last = 2 * (rows + 2) * pitch
    taken[last : last + EDGE, 3 * depth :] = jnp.zeros((EDGE, depth), jnp.bfloat16)

    lines = 2 * rows
    total = (lines + 2) * pitch + EDGE
    even[0:EDGE] = jnp.zeros((EDGE, depth), jnp.float32)
    odd[0:EDGE] = jnp.zeros((EDGE, depth), jnp.float32)
    even[EDGE + total :] = jnp.zeros((EDGE, depth), jnp.float32)
    odd[EDGE + total :] = jnp.zeros((EDGE, depth), jnp.float32)

    def taps(source, kernel, at, size, q):
        found = None
        for r in range(3):
            part = jnp.dot(
                source[pl.ds(at + r * pitch, size), q * depth : (q + 3) * depth], kernel[r],
                preferred_element_type=jnp.float32,
            )
            found = part if found is None else found + part
        return found

    pieces = 3
    step = -(-total // pieces // EDGE) * EDGE
    for at in range(0, total, step):
        size = min(step, total - at)
        kept = keep[at : at + size, :] > 0.0
        kept = jnp.concatenate([kept] * (depth // LANES), axis=1)
        for q, held in ((0, even), (1, odd)):
            value = taps(taken, first_kernel, at, size, q) + first_bias[...]
            value = jax.nn.gelu(value)
            held[EDGE + at : EDGE + at + size] = jnp.where(kept, value, 0.0)
    acted[:, depth : 2 * depth] = even[EDGE : EDGE + total].astype(jnp.bfloat16)
    acted[:, 2 * depth : 3 * depth] = odd[EDGE : EDGE + total].astype(jnp.bfloat16)
    acted[:, 0:depth] = odd[EDGE - 1 : EDGE - 1 + total].astype(jnp.bfloat16)
    acted[:, 3 * depth :] = even[EDGE + 1 : EDGE + 1 + total].astype(jnp.bfloat16)

    group = max(lines // 4, 1)
    for at in range(0, lines, group):
        size = group * pitch - EDGE
        for q in range(2):
            value = taps(acted, second_kernel, EDGE + at * pitch, size, q) + second_bias[...]
            for y in range(group):
                for lane in range(depth // LANES):
                    woven[lane, pl.ds((at + y) * 2 * cols + q, cols, stride=2), :] = value[
                        y * pitch : y * pitch + cols, lane * LANES : (lane + 1) * LANES
                    ]
    for lane in range(depth // LANES):
        out[:, lane * LANES : (lane + 1) * LANES] = woven[lane].astype(jnp.bfloat16)


def convolve_twice(outer, middle, above, below, left, right, keep, first_kernel, first_bias, second_kernel, second_bias):
    rows, cols, width = (2 * outer.shape[0],) + outer.shape[1:]
    pitch = cols + EDGE
    total = (2 * rows + 2) * pitch + EDGE
    depth = CHANNELS
    found = pl.pallas_call(
        functools.partial(conv_kernel, rows, cols),
        out_shape=jax.ShapeDtypeStruct((4 * rows * cols, depth), jnp.bfloat16),
        in_specs=[pl.BlockSpec(memory_space=pltpu.VMEM)] * 11,
        out_specs=pl.BlockSpec(memory_space=pltpu.VMEM),
        scratch_shapes=[
            pltpu.VMEM(((2 * rows + 4) * pitch + EDGE, 4 * depth), jnp.bfloat16),
            pltpu.VMEM((total + 2 * EDGE, depth), jnp.float32),
            pltpu.VMEM((total + 2 * EDGE, depth), jnp.float32),
            pltpu.VMEM((total, 4 * depth), jnp.bfloat16),
            pltpu.VMEM((depth // LANES, 4 * rows * cols, LANES), jnp.float32),
        ],
        compiler_params=params(),
    )(
        outer.reshape(-1, width), middle.reshape(-1, width), above, below, left, right, keep,
        first_kernel.reshape(3, 3 * depth, depth), first_bias.reshape(1, depth),
        second_kernel.reshape(3, 3 * depth, depth), second_bias.reshape(1, depth),
    )
    return found.reshape(2 * rows, 2 * cols, depth)


def kept_rows(rows, cols):
    pitch = cols + EDGE
    lines = 2 * rows
    total = (lines + 2) * pitch + EDGE
    row, col = lax.axis_index("row"), lax.axis_index("col")
    top, bottom = row == 0, row == lax.axis_size("row") - 1
    start, end = col == 0, col == lax.axis_size("col") - 1
    flat = jnp.arange(total)
    line, place = flat // pitch - 1, flat % pitch - EDGE
    wrapped = place == -EDGE
    line = jnp.where(wrapped, line - 1, line)
    place = jnp.where(wrapped, cols, place)
    outside = (
        ((line < 0) & top) | ((line >= lines) & bottom)
        | ((place < 0) & start) | ((place >= cols) & end)
    )
    return jnp.broadcast_to(jnp.where(outside, 0.0, 1.0)[:, None], (total, LANES)).astype(jnp.float32)


def shifted(value, axis, by):
    size = lax.axis_size(axis)
    pairs = [(i, i + by) for i in range(size) if 0 <= i + by < size]
    return lax.ppermute(value, axis, pairs)


def across(value, axis, by, unit=1):
    size = lax.axis_size(axis)
    return lax.ppermute(value, axis, [(i, (i + by * unit) % size) for i in range(size)])


def paired(value, axis):
    return lax.ppermute(value, axis, [(i, i ^ 1) for i in range(lax.axis_size(axis))])


def picked(value, index, axis=0):
    return lax.dynamic_index_in_dim(value, index, axis, keepdims=False)


def shards(
    query_window, key_window, value_window, query_index, key_index,
    proj_weight, proj_bias, first_kernel, first_bias, second_kernel, second_bias,
):
    rows_dev, cols_dev, tokens_win, features = query_window.shape
    windows = rows_dev * cols_dev
    flat = (windows, tokens_win, features)
    inner, cores = 2, lax.axis_size("col")
    outer = lax.axis_size("row") // inner
    row, core = lax.axis_index("row"), lax.axis_index("col")
    z, y = row // inner, row % inner
    chunk = tokens_win // 2
    owned = chunk // (outer * inner)
    slab = inner * owned
    half = features // cores

    def slab_of(value, part, place):
        at = place * slab
        if part == 0:
            at = jnp.where(at < chunk // 2, at, at + chunk)
        else:
            at = at + chunk // 2
        cut = lax.dynamic_slice_in_dim(value, at, slab, axis=value.ndim - 2)
        return cut.reshape(cut.shape[:-2] + (inner, owned, cut.shape[-1]))

    query, key_rows = query_index.reshape(flat), key_index.reshape(flat)
    sent = []
    for k in range(outer):
        place = (z + k) % outer
        block = jnp.stack(
            [slab_of(value, part, place) for part in range(2) for value in (query, key_rows)]
        )
        sent.append(across(block, "row", k, inner) if k else block)
    near = [picked(block, y, 2) for block in sent]
    far = [paired(picked(block, 1 - y, 2), "row") for block in sent]
    pair = jnp.stack([jnp.stack([a, b], axis=1) for a, b in zip(near, far)], axis=1)
    pair = pair.reshape(2, 2, -1, features)
    own_half = lax.dynamic_slice_in_dim(pair, core * half, half, axis=3)
    other_half = lax.dynamic_slice_in_dim(pair, (1 - core) * half, half, axis=3)
    weights = []
    for part in range(2):
        here, there = own_half[part], paired(other_half[part], "col")
        weights.append(index_weights(here[0], there[0], here[1], there[1], owned))

    window_out = window_attend(
        query_window.reshape(flat), key_window.reshape(flat), value_window.reshape(flat), cores
    )
    window_out = jnp.stack([picked(window_out, core), paired(picked(window_out, 1 - core), "col")])
    ordered = jnp.concatenate([proj_weight, proj_weight], axis=0)
    ordered = lax.dynamic_slice_in_dim(ordered, core * half, features, axis=0)
    keep = kept_rows(rows_dev * TILE_ROWS, cols_dev * TILE_COLS)

    images = []
    for part in range(2):
        blocks = jnp.stack([slab_of(window_out, part, (z + k) % outer) for k in range(outer)])
        here, there = picked(blocks, y, 3), paired(picked(blocks, 1 - y, 3), "row")
        pieces = []
        for k in range(outer):
            piece = jnp.stack([here[k], there[k]]).reshape(inner, cores, windows * owned, half)
            pieces.append(across(piece, "row", k, inner) if k else piece)
        mixed_near, mixed_far = index_mix(weights[part], pieces)
        projected = project(mixed_near, paired(mixed_far, "col"), ordered, proj_bias)
        width = projected.shape[-1]
        projected = projected.reshape(outer, inner, windows, owned, width)
        here, there = projected[:, 0], paired(projected[:, 1], "row")
        returned = []
        for k in range(outer):
            piece = jnp.stack([here[k], there[k]])
            returned.append(across(piece, "row", -k, inner) if k else piece)
        returned = jnp.stack(returned)
        placed = jnp.stack([picked(returned, (place - z) % outer) for place in range(outer)])
        placed = jnp.where(y == 0, placed, placed[:, ::-1])
        tokens = jnp.transpose(placed, (2, 0, 1, 3, 4)).reshape(
            rows_dev, cols_dev, TILE_ROWS // 2, TILE_COLS, width
        )
        images.append(
            jnp.transpose(tokens, (0, 2, 1, 3, 4)).reshape(-1, cols_dev * TILE_COLS, width)
        )
    image_outer, image_middle = images
    above = shifted(image_outer[-1:], "row", 1)
    below = shifted(image_outer[:1], "row", -1)
    quarter = image_outer.shape[0] // 2

    def column(at):
        return jnp.concatenate(
            [
                above[:, at], image_outer[:quarter, at], image_middle[:, at],
                image_outer[quarter:, at], below[:, at],
            ],
            axis=0,
        )

    left = shifted(column(-1), "col", 1)
    right = shifted(column(0), "col", -1)
    return convolve_twice(
        image_outer, image_middle, above[0], below[0], left, right, keep,
        first_kernel, first_bias, second_kernel, second_bias,
    )


def solution(mesh):
    spread = P(("grp", "row"), "col", None, None)
    in_specs = (spread,) * 5 + (P(),) * 6
    out_specs = P(("grp", "row"), "col", None)
    return jax.shard_map(shards, mesh=mesh, in_specs=in_specs, out_specs=out_specs, check_vma=False)
```

```python
import functools
import math

import jax
import jax.numpy as jnp
from jax import lax
from jax.experimental import pallas as pl
from jax.experimental.pallas import tpu as pltpu
from jax.sharding import PartitionSpec as P

HEADS = 8
HEAD_DIM = 160
CHANNELS = 256
TILE_ROWS = 8
TILE_COLS = 16
LANES = 128
EDGE = 16
PIECE = 8
SPAN = 2 * LANES
VMEM_BYTES = 40 * 1024 * 1024


def params(steps=0):
    return pltpu.CompilerParams(
        dimension_semantics=("arbitrary",) * steps if steps else None,
        vmem_limit_bytes=VMEM_BYTES,
    )


def head_start(head):
    return head * HEAD_DIM // LANES * LANES


def head_mask(head):
    lane = lax.broadcasted_iota(jnp.int32, (1, SPAN), 1) + head_start(head)
    return (lane >= head * HEAD_DIM) & (lane < (head + 1) * HEAD_DIM)


def joined_heads(mixed):
    tiles = []
    lane = lax.broadcasted_iota(jnp.int32, (1, LANES), 1)
    for tile in range(len(mixed) * HEAD_DIM // LANES):
        base = tile * LANES
        first, last = base // HEAD_DIM, (base + LANES - 1) // HEAD_DIM
        pieces = []
        for head in (first, last):
            at = base - head_start(head)
            pieces.append(mixed[head][:, at : at + LANES])
        if first == last:
            tiles.append(pieces[0])
        else:
            tiles.append(jnp.where(lane < last * HEAD_DIM - base, pieces[0], pieces[1]))
    return jnp.concatenate(tiles, axis=1)


def softmax_rows(scores):
    raised = jnp.exp(scores - jnp.max(scores, axis=-1, keepdims=True))
    return (raised / jnp.sum(raised, axis=-1, keepdims=True)).astype(jnp.bfloat16)


def window_kernel(query, key_rows, value, out):
    mixed = []
    for head in range(HEADS):
        lanes = pl.ds(head_start(head), SPAN)
        masked = jnp.where(head_mask(head), query[0, :, lanes], 0)
        scores = lax.dot_general(
            masked, key_rows[0, :, lanes], (((1,), (1,)), ((), ())),
            preferred_element_type=jnp.float32,
        ) * (1.0 / math.sqrt(HEAD_DIM))
        mixed.append(
            jnp.dot(softmax_rows(scores), value[0, :, lanes], preferred_element_type=jnp.float32)
        )
    joined = joined_heads(mixed).astype(jnp.bfloat16)
    parts, features = out.shape[0], out.shape[-1]
    for part in range(parts):
        out[part, 0] = joined[:, part * features : (part + 1) * features]


def window_attend(query, key_rows, value, parts):
    windows, tokens, features = query.shape
    result = (parts, windows, tokens, features // parts)
    block = pl.BlockSpec((1, tokens, features), lambda w: (w, 0, 0))
    return pl.pallas_call(
        window_kernel,
        grid=(windows,),
        in_specs=[block] * 3,
        out_specs=pl.BlockSpec((parts, 1, tokens, features // parts), lambda w: (0, w, 0, 0)),
        out_shape=jax.ShapeDtypeStruct(result, jnp.bfloat16),
        compiler_params=params(1),
    )(query, key_rows, value)


def token_of(place, part, owned, places):
    chunk = owned * places
    if part:
        return chunk // 2 + place * owned
    return place * owned if place * owned < chunk // 2 else chunk + place * owned


def deal_kernel(query, key_rows, out, held, packed, arrived, left):
    places, cores, parts, kinds, block, half = out.shape
    windows = query.shape[0]
    owned = block // windows
    copies = [
        pltpu.make_async_copy(source, held.at[kind], arrived.at[kind])
        for kind, source in enumerate((query, key_rows))
    ]
    for copy in copies:
        copy.start()
    for copy in copies:
        copy.wait()
    copies = []
    for place in range(places):
        for part in range(parts):
            rows = pl.ds(token_of(place, part, owned, places), owned)
            for kind in range(kinds):
                for window in range(windows):
                    for core in range(cores):
                        packed[place, core, part, kind, pl.ds(window * owned, owned), :] = held[
                            kind, window, rows, core * half : (core + 1) * half
                        ]
        copy = pltpu.make_async_copy(packed.at[place], out.at[place], left.at[place])
        copy.start()
        copies.append(copy)
    for copy in copies:
        copy.wait()


def dealt(query, key_rows, places, cores):
    windows, tokens, features = query.shape
    result = (places, cores, 2, 2, windows * tokens // (2 * places), features // cores)
    return pl.pallas_call(
        deal_kernel,
        in_specs=[pl.BlockSpec(memory_space=pltpu.HBM)] * 2,
        out_specs=pl.BlockSpec(memory_space=pltpu.HBM),
        out_shape=pltpu.HBM(result, query.dtype),
        scratch_shapes=[
            pltpu.VMEM((2,) + query.shape, query.dtype),
            pltpu.VMEM(result, query.dtype),
            pltpu.SemaphoreType.DMA((2,)),
            pltpu.SemaphoreType.DMA((places,)),
        ],
        compiler_params=params(),
    )(
        pltpu.with_memory_space_constraint(query, pltpu.HBM),
        pltpu.with_memory_space_constraint(key_rows, pltpu.HBM),
    )


def weights_kernel(tokens, core, pair, out):
    places, cores, _, _, block, _ = pair.shape
    head = pl.program_id(0)
    start = head * HEAD_DIM // LANES * LANES
    lanes = pl.ds(pl.multiple_of(start, LANES), SPAN)
    lane = lax.broadcasted_iota(jnp.int32, (1, SPAN), 1) + start
    inside = (lane >= head * HEAD_DIM) & (lane < (head + 1) * HEAD_DIM)
    held = jnp.float32 if block % EDGE else jnp.bfloat16

    def gathered(kind):
        return jnp.concatenate(
            [
                pair[place, core[0] ^ far, 0, kind, :, lanes].astype(held)
                for far in range(cores)
                for place in range(places)
            ],
            axis=0,
        ).astype(jnp.bfloat16)

    scores = lax.dot_general(
        jnp.where(inside, gathered(0), 0), gathered(1), (((1,), (1,)), ((), ())),
        preferred_element_type=jnp.float32,
    ) * (1.0 / math.sqrt(HEAD_DIM))
    rows = scores.shape[0]
    token_row = lax.broadcasted_iota(jnp.int32, (rows, 1), 0) % tokens
    token_col = lax.broadcasted_iota(jnp.int32, (1, rows), 1) % tokens
    out[0] = softmax_rows(jnp.where(token_row == token_col, scores, -jnp.inf))


def index_weights(core, pair, part, tokens):
    places, cores, _, kinds, block, features = pair.shape
    heads = features // HEAD_DIM
    rows = places * cores * block
    return pl.pallas_call(
        functools.partial(weights_kernel, tokens),
        grid=(heads,),
        in_specs=[
            pl.BlockSpec(memory_space=pltpu.SMEM),
            pl.BlockSpec((places, cores, 1, kinds, block, features), lambda h: (0, 0, part, 0, 0, 0)),
        ],
        out_specs=pl.BlockSpec((1, rows, rows), lambda h: (h, 0, 0)),
        out_shape=jax.ShapeDtypeStruct((heads, rows, rows), jnp.bfloat16),
        compiler_params=params(1),
    )(core.reshape(1), pair)


def mix_kernel(place, weights, *refs):
    pieces, (near, far, value) = refs[:-3], refs[-3:]
    inner, cores, rows, features = pieces[0].shape
    half = value.shape[0] // cores
    for k, piece in enumerate(pieces):
        for j in range(inner):
            at = pl.multiple_of((place[0] ^ (k * inner + j)) * rows, rows)
            for core in range(cores):
                value[pl.ds(core * half + at, rows), :] = piece[j, core].astype(value.dtype)
    mixed = []
    for head in range(features // HEAD_DIM):
        lanes = slice(head_start(head), head_start(head) + SPAN)
        mixed.append(
            jnp.dot(
                weights[head], value[:, lanes].astype(jnp.bfloat16),
                preferred_element_type=jnp.float32,
            )
        )
    joined = joined_heads(mixed).astype(jnp.bfloat16)
    near[...] = joined[:half]
    far[...] = joined[half:]


def index_mix(place, weights, pieces):
    rows, features = weights.shape[1], pieces[0].shape[-1]
    result = jax.ShapeDtypeStruct((rows // 2, features), jnp.bfloat16)
    held = jnp.float32 if pieces[0].shape[2] % EDGE else jnp.bfloat16
    return pl.pallas_call(
        mix_kernel,
        in_specs=[pl.BlockSpec(memory_space=pltpu.SMEM)]
        + [pl.BlockSpec(memory_space=pltpu.VMEM)] * (1 + len(pieces)),
        out_specs=[pl.BlockSpec(memory_space=pltpu.VMEM)] * 2,
        out_shape=[result, result],
        scratch_shapes=[pltpu.VMEM((rows, features), held)],
        compiler_params=params(),
    )(place.reshape(1), weights, *pieces)


def project_kernel(core, near, far, proj_weight, proj_bias, out):
    half = near.shape[1]
    total = proj_bias[...]
    for held, place in ((near, core[0]), (far, 1 - core[0])):
        rows = pl.ds(pl.multiple_of(place * half, half), half)
        total = total + jnp.dot(held[...], proj_weight[rows, :], preferred_element_type=jnp.float32)
    out[...] = total.astype(jnp.bfloat16)


def project(near, far, proj_weight, proj_bias, core):
    return pl.pallas_call(
        project_kernel,
        in_specs=[pl.BlockSpec(memory_space=pltpu.SMEM)]
        + [pl.BlockSpec(memory_space=pltpu.VMEM)] * 4,
        out_specs=pl.BlockSpec(memory_space=pltpu.VMEM),
        out_shape=pltpu.HBM((near.shape[0], proj_weight.shape[1]), jnp.bfloat16),
        compiler_params=params(),
    )(core.reshape(1), near, far, proj_weight, proj_bias.reshape(1, -1))


def line_of(line, rows):
    quarter = rows // 4
    if line < quarter:
        return 0, line
    if line < 3 * quarter:
        return 1, line - quarter
    return 0, line - 2 * quarter


def conv_kernel(
    rows, cols, outer, middle, above, below, left, right, keep,
    first_kernel, first_bias, second_kernel, second_bias, out,
    taken, even, odd, acted, woven,
):
    pitch = cols + EDGE
    depth = CHANNELS
    place = lax.broadcasted_iota(jnp.int32, (EDGE, 1), 0)
    half = 2 * depth

    def gap_of(row):
        block = jnp.zeros((EDGE, half), jnp.float32)
        if row >= 1:
            token, sub = (row - 1) // 2, (row - 1) % 2
            block = jnp.where(
                place == 0,
                right[token : token + 1, sub * half : (sub + 1) * half].astype(jnp.float32),
                block,
            )
        if row < 2 * (rows + 2):
            token, sub = row // 2, row % 2
            block = jnp.where(
                place == EDGE - 1,
                left[token : token + 1, sub * half : (sub + 1) * half].astype(jnp.float32),
                block,
            )
        return block

    taken[0:EDGE, 0:depth] = jnp.zeros((EDGE, depth), jnp.bfloat16)
    for i in range(rows + 2):
        if i == 0:
            source, at = above, 0
        elif i == rows + 1:
            source, at = below, 0
        else:
            part, at = line_of(i - 1, rows)
            source = (outer, middle)[part]
        _, windows, piece, _ = source.shape
        per = TILE_COLS // piece
        body = jnp.concatenate(
            [
                source[at * per + across, window].astype(jnp.float32)
                for window in range(windows)
                for across in range(per)
            ],
            axis=0,
        )
        for p in range(2):
            lanes = slice(p * half, (p + 1) * half)
            y = 2 * i + p
            line = jnp.concatenate([gap_of(y), body[:, lanes], gap_of(y + 1)], axis=0)
            length = line.shape[0]
            base = y * pitch
            taken[base : base + length, depth : 3 * depth] = line.astype(jnp.bfloat16)
            later = pltpu.roll(line[:, depth:], 1, 0)
            sooner = pltpu.roll(line[:, :depth], length - 1, 0)
            taken[base + EDGE : base + length, 0:depth] = later[EDGE:].astype(jnp.bfloat16)
            taken[base : base + pitch, 3 * depth :] = sooner[:pitch].astype(jnp.bfloat16)
    last = 2 * (rows + 2) * pitch
    taken[last : last + EDGE, 3 * depth :] = jnp.zeros((EDGE, depth), jnp.bfloat16)

    lines = 2 * rows
    total = (lines + 2) * pitch + EDGE
    even[0:EDGE] = jnp.zeros((EDGE, depth), jnp.float32)
    odd[0:EDGE] = jnp.zeros((EDGE, depth), jnp.float32)
    even[EDGE + total :] = jnp.zeros((EDGE, depth), jnp.float32)
    odd[EDGE + total :] = jnp.zeros((EDGE, depth), jnp.float32)

    def taps(source, kernel, at, size, q):
        found = None
        for r in range(3):
            part = jnp.dot(
                source[pl.ds(at + r * pitch, size), q * depth : (q + 3) * depth], kernel[r],
                preferred_element_type=jnp.float32,
            )
            found = part if found is None else found + part
        return found

    pieces = 3
    step = -(-total // pieces // EDGE) * EDGE
    for at in range(0, total, step):
        size = min(step, total - at)
        kept = keep[at : at + size, :] > 0.0
        kept = jnp.concatenate([kept] * (depth // LANES), axis=1)
        for q, held in ((0, even), (1, odd)):
            value = taps(taken, first_kernel, at, size, q) + first_bias[...]
            value = jax.nn.gelu(value)
            held[EDGE + at : EDGE + at + size] = jnp.where(kept, value, 0.0)
    acted[:, depth : 2 * depth] = even[EDGE : EDGE + total].astype(jnp.bfloat16)
    acted[:, 2 * depth : 3 * depth] = odd[EDGE : EDGE + total].astype(jnp.bfloat16)
    acted[:, 0:depth] = odd[EDGE - 1 : EDGE - 1 + total].astype(jnp.bfloat16)
    acted[:, 3 * depth :] = even[EDGE + 1 : EDGE + 1 + total].astype(jnp.bfloat16)

    group = max(lines // 4, 1)
    for at in range(0, lines, group):
        size = group * pitch - EDGE
        for q in range(2):
            value = taps(acted, second_kernel, EDGE + at * pitch, size, q) + second_bias[...]
            for y in range(group):
                for lane in range(depth // LANES):
                    woven[lane, pl.ds((at + y) * 2 * cols + q, cols, stride=2), :] = value[
                        y * pitch : y * pitch + cols, lane * LANES : (lane + 1) * LANES
                    ]
    for lane in range(depth // LANES):
        out[:, lane * LANES : (lane + 1) * LANES] = woven[lane].astype(jnp.bfloat16)


def convolve_twice(outer, middle, above, below, left, right, keep, first_kernel, first_bias, second_kernel, second_bias):
    pieces, windows, piece, _ = outer.shape
    rows, cols = 2 * pieces * piece // TILE_COLS, windows * TILE_COLS
    pitch = cols + EDGE
    total = (2 * rows + 2) * pitch + EDGE
    depth = CHANNELS
    found = pl.pallas_call(
        functools.partial(conv_kernel, rows, cols),
        out_shape=jax.ShapeDtypeStruct((4 * rows * cols, depth), jnp.bfloat16),
        in_specs=[pl.BlockSpec(memory_space=pltpu.VMEM)] * 11,
        out_specs=pl.BlockSpec(memory_space=pltpu.VMEM),
        scratch_shapes=[
            pltpu.VMEM(((2 * rows + 4) * pitch + EDGE, 4 * depth), jnp.bfloat16),
            pltpu.VMEM((total + 2 * EDGE, depth), jnp.float32),
            pltpu.VMEM((total + 2 * EDGE, depth), jnp.float32),
            pltpu.VMEM((total, 4 * depth), jnp.bfloat16),
            pltpu.VMEM((depth // LANES, 4 * rows * cols, LANES), jnp.float32),
        ],
        compiler_params=params(),
    )(
        outer, middle, above, below, left, right, keep,
        first_kernel.reshape(3, 3 * depth, depth), first_bias.reshape(1, depth),
        second_kernel.reshape(3, 3 * depth, depth), second_bias.reshape(1, depth),
    )
    return found.reshape(2 * rows, 2 * cols, depth)


def kept_rows(rows, cols):
    pitch = cols + EDGE
    lines = 2 * rows
    total = (lines + 2) * pitch + EDGE
    row, col = lax.axis_index("row"), lax.axis_index("col")
    top, bottom = row == 0, row == lax.axis_size("row") - 1
    start, end = col == 0, col == lax.axis_size("col") - 1
    flat = jnp.arange(total)
    line, place = flat // pitch - 1, flat % pitch - EDGE
    wrapped = place == -EDGE
    line = jnp.where(wrapped, line - 1, line)
    place = jnp.where(wrapped, cols, place)
    outside = (
        ((line < 0) & top) | ((line >= lines) & bottom)
        | ((place < 0) & start) | ((place >= cols) & end)
    )
    return jnp.broadcast_to(jnp.where(outside, 0.0, 1.0)[:, None], (total, LANES)).astype(jnp.float32)


def shifted(value, axis, by):
    size = lax.axis_size(axis)
    pairs = [(i, i + by) for i in range(size) if 0 <= i + by < size]
    return lax.ppermute(value, axis, pairs)


def swapped(value, axis, by):
    return lax.ppermute(value, axis, [(i, i ^ by) for i in range(lax.axis_size(axis))])


def exchanged(value, axes):
    return lax.all_to_all(value, axes, split_axis=0, concat_axis=0, tiled=True)


def in_pieces(value):
    places, windows, owned, width = value.shape
    if owned < PIECE:
        joined = value.reshape(-1, PIECE // owned, windows, owned, width)
        return jnp.swapaxes(joined, 1, 2).reshape(-1, windows, PIECE, width)
    cut = value.reshape(places, windows, owned // PIECE, PIECE, width)
    return jnp.swapaxes(cut, 1, 2).reshape(-1, windows, PIECE, width)


def picked(value, index, axis=0):
    return lax.dynamic_index_in_dim(value, index, axis, keepdims=False)


def after(value, *earlier):
    return lax.optimization_barrier((value,) + earlier)[0]


def shards(
    query_window, key_window, value_window, query_index, key_index,
    proj_weight, proj_bias, first_kernel, first_bias, second_kernel, second_bias,
):
    rows_dev, cols_dev, tokens_win, features = query_window.shape
    windows = rows_dev * cols_dev
    flat = (windows, tokens_win, features)
    inner, cores, places = 2, lax.axis_size("col"), lax.axis_size("row")
    outer = places // inner
    row, core = lax.axis_index("row"), lax.axis_index("col")
    z, y = row // inner, row % inner
    chunk = tokens_win // 2
    owned = chunk // places
    half = features // cores

    def slab_of(value, part, place, count):
        at = place * owned
        if part == 0:
            at = jnp.where(at < chunk // 2, at, at + chunk)
        else:
            at = at + chunk // 2
        cut = lax.dynamic_slice_in_dim(value, at, count * owned, axis=value.ndim - 2)
        return cut.reshape(cut.shape[:-2] + (count, owned, cut.shape[-1]))

    query, key_rows = query_index.reshape(flat), key_index.reshape(flat)
    pair = exchanged(
        dealt(query, key_rows, places, cores).reshape(places * cores, 2, 2, windows * owned, half),
        ("row", "col"),
    ).reshape(places, cores, 2, 2, windows * owned, half)

    window_out = window_attend(
        query_window.reshape(flat), key_window.reshape(flat),
        value_window.reshape(flat), cores,
    )
    window_out = jnp.stack([picked(window_out, core), swapped(picked(window_out, 1 - core), "col", 1)])
    blocks = jnp.stack(
        [
            jnp.stack([slab_of(window_out, part, (z ^ k) * inner, inner) for part in range(2)])
            for k in range(outer)
        ]
    )
    values_near, values_far = picked(blocks, y, 4), swapped(picked(blocks, 1 - y, 4), "row", 1)
    weights = [index_weights(core, pair, part, owned) for part in range(2)]
    keep = kept_rows(rows_dev * TILE_ROWS, cols_dev * TILE_COLS)

    images = []
    earlier = []
    pieces = []
    for part in range(2):
        pieces.append([])
        for k in range(outer):
            piece = jnp.stack([values_near[k, part], values_far[k, part]])
            piece = piece.reshape(inner, cores, windows * owned, half)
            pieces[part].append(swapped(piece, "row", k * inner) if k else piece)
    for part in range(2):
        mixed_near, mixed_far = index_mix(row, after(weights[part], *earlier), pieces[part])
        projected = project(mixed_near, swapped(mixed_far, "col", 1), proj_weight, proj_bias, core)
        width = projected.shape[-1]
        earlier = [projected]
        if not part:
            projected = after(projected, *pieces[1])
        returned = in_pieces(exchanged(projected.reshape(places, windows, owned, width), "row"))
        line = TILE_COLS // PIECE
        if part:
            above = shifted(after(images[0][-line:], projected), "row", 1)
            below = shifted(after(images[0][:line], projected), "row", -1)
            returned = after(returned, above, below)
        images.append(returned)
    outer_rows, middle_rows = images
    half_way = outer_rows.shape[0] // 2

    def column(first):
        window, token = (0, 0) if first else (-1, -1)
        start = 0 if first else line - 1
        return jnp.concatenate(
            [
                lines[start::line, window, token]
                for lines in (
                    above, outer_rows[:half_way], middle_rows, outer_rows[half_way:], below
                )
            ],
            axis=0,
        )

    if cores == 2:
        other = swapped(jnp.where(core == 0, column(False), column(True)), "col", 1)
        left = jnp.where(core == 1, other, 0)
        right = jnp.where(core == 0, other, 0)
    else:
        left, right = shifted(column(False), "col", 1), shifted(column(True), "col", -1)
    return convolve_twice(
        outer_rows, middle_rows, above, below, left, right, keep,
        first_kernel, first_bias, second_kernel, second_bias,
    )


def solution(mesh):
    spread = P(("grp", "row"), "col", None, None)
    in_specs = (spread,) * 5 + (P(),) * 6
    out_specs = P(("grp", "row"), "col", None)
    return jax.shard_map(shards, mesh=mesh, in_specs=in_specs, out_specs=out_specs, check_vma=False)
```

```python
import functools
import math

import jax
import jax.numpy as jnp
from jax import lax
from jax.experimental import pallas as pl
from jax.experimental.pallas import tpu as pltpu
from jax.sharding import PartitionSpec as P

HEADS = 8
HEAD_DIM = 160
CHANNELS = 256
TILE_ROWS = 8
TILE_COLS = 16
LANES = 128
EDGE = 16
PIECE = 8
SPAN = 2 * LANES
VMEM_BYTES = 16 * 1024 * 1024


def params(steps=0, size=VMEM_BYTES):
    return pltpu.CompilerParams(
        dimension_semantics=("arbitrary",) * steps if steps else None,
        vmem_limit_bytes=size,
    )


def head_start(head):
    return head * HEAD_DIM // LANES * LANES


def head_mask(head):
    lane = lax.broadcasted_iota(jnp.int32, (1, SPAN), 1) + head_start(head)
    return (lane >= head * HEAD_DIM) & (lane < (head + 1) * HEAD_DIM)


def joined_heads(mixed):
    tiles = []
    lane = lax.broadcasted_iota(jnp.int32, (1, LANES), 1)
    for tile in range(len(mixed) * HEAD_DIM // LANES):
        base = tile * LANES
        first, last = base // HEAD_DIM, (base + LANES - 1) // HEAD_DIM
        pieces = []
        for head in (first, last):
            at = base - head_start(head)
            pieces.append(mixed[head][:, at : at + LANES])
        if first == last:
            tiles.append(pieces[0])
        else:
            tiles.append(jnp.where(lane < last * HEAD_DIM - base, pieces[0], pieces[1]))
    return jnp.concatenate(tiles, axis=1)


def softmax_rows(scores):
    raised = jnp.exp(scores - jnp.max(scores, axis=-1, keepdims=True))
    return (raised / jnp.sum(raised, axis=-1, keepdims=True)).astype(jnp.bfloat16)


def window_kernel(query, key_rows, value, out):
    mixed = []
    for head in range(HEADS):
        lanes = pl.ds(head_start(head), SPAN)
        masked = jnp.where(head_mask(head), query[0, :, lanes], 0)
        scores = lax.dot_general(
            masked, key_rows[0, :, lanes], (((1,), (1,)), ((), ())),
            preferred_element_type=jnp.float32,
        ) * (1.0 / math.sqrt(HEAD_DIM))
        mixed.append(
            jnp.dot(softmax_rows(scores), value[0, :, lanes], preferred_element_type=jnp.float32)
        )
    joined = joined_heads(mixed).astype(jnp.bfloat16)
    parts, features = out.shape[0], out.shape[-1]
    for part in range(parts):
        out[part, 0] = joined[:, part * features : (part + 1) * features]


def window_attend(query, key_rows, value, parts):
    windows, tokens, features = query.shape
    result = (parts, windows, tokens, features // parts)
    block = pl.BlockSpec((1, tokens, features), lambda w: (w, 0, 0))
    return pl.pallas_call(
        window_kernel,
        grid=(windows,),
        in_specs=[block] * 3,
        out_specs=pl.BlockSpec((parts, 1, tokens, features // parts), lambda w: (0, w, 0, 0)),
        out_shape=jax.ShapeDtypeStruct(result, jnp.bfloat16),
        compiler_params=params(1),
    )(query, key_rows, value)


def token_of(place, part, owned, places):
    chunk = owned * places
    if part:
        return chunk // 2 + place * owned
    return place * owned if place * owned < chunk // 2 else chunk + place * owned


def deal_kernel(query, key_rows, out, held, packed, arrived, left):
    places, cores, parts, kinds, block, half = out.shape
    windows = query.shape[0]
    owned = block // windows
    arriving = [
        pltpu.make_async_copy(source, held.at[kind], arrived.at[kind])
        for kind, source in enumerate((query, key_rows))
    ]
    for copy in arriving:
        copy.start()
    leaving = []
    for kind in range(kinds):
        arriving[kind].wait()
        for place in range(places):
            for part in range(parts):
                rows = pl.ds(token_of(place, part, owned, places), owned)
                for window in range(windows):
                    for core in range(cores):
                        packed[kind, place, core, part, pl.ds(window * owned, owned), :] = held[
                            kind, window, rows, core * half : (core + 1) * half
                        ]
        copy = pltpu.make_async_copy(packed.at[kind], out.at[:, :, :, kind], left.at[kind])
        copy.start()
        leaving.append(copy)
    for copy in leaving:
        copy.wait()


def dealt(query, key_rows, places, cores):
    windows, tokens, features = query.shape
    result = (places, cores, 2, 2, windows * tokens // (2 * places), features // cores)
    return pl.pallas_call(
        deal_kernel,
        in_specs=[pl.BlockSpec(memory_space=pltpu.HBM)] * 2,
        out_specs=pl.BlockSpec(memory_space=pltpu.HBM),
        out_shape=pltpu.HBM(result, query.dtype),
        scratch_shapes=[
            pltpu.VMEM((2,) + query.shape, query.dtype),
            pltpu.VMEM((2,) + result[:3] + result[4:], query.dtype),
            pltpu.SemaphoreType.DMA((2,)),
            pltpu.SemaphoreType.DMA((2,)),
        ],
        compiler_params=params(),
    )(
        pltpu.with_memory_space_constraint(query, pltpu.HBM),
        pltpu.with_memory_space_constraint(key_rows, pltpu.HBM),
    )


def weights_kernel(tokens, core, pair, *outs):
    places, cores, _, _, block, _ = pair.shape
    head = pl.program_id(1)
    start = head * HEAD_DIM // LANES * LANES
    lanes = pl.ds(pl.multiple_of(start, LANES), SPAN)
    lane = lax.broadcasted_iota(jnp.int32, (1, SPAN), 1) + start
    inside = (lane >= head * HEAD_DIM) & (lane < (head + 1) * HEAD_DIM)
    held = jnp.float32 if block % EDGE else jnp.bfloat16

    def gathered(kind):
        return jnp.concatenate(
            [
                pair[place, core[0] ^ far, 0, kind, :, lanes].astype(held)
                for far in range(cores)
                for place in range(places)
            ],
            axis=0,
        ).astype(jnp.bfloat16)

    scores = lax.dot_general(
        jnp.where(inside, gathered(0), 0), gathered(1), (((1,), (1,)), ((), ())),
        preferred_element_type=jnp.float32,
    ) * (1.0 / math.sqrt(HEAD_DIM))
    rows = scores.shape[0]
    token_row = lax.broadcasted_iota(jnp.int32, (rows, 1), 0) % tokens
    token_col = lax.broadcasted_iota(jnp.int32, (1, rows), 1) % tokens
    found = softmax_rows(jnp.where(token_row == token_col, scores, -jnp.inf))
    for part, out in enumerate(outs):

        @pl.when(pl.program_id(0) == part)
        def _(out=out):
            out[0] = found


def index_weights(core, pair, tokens):
    places, cores, parts, kinds, block, features = pair.shape
    heads = features // HEAD_DIM
    rows = places * cores * block
    return pl.pallas_call(
        functools.partial(weights_kernel, tokens),
        grid=(parts, heads),
        in_specs=[
            pl.BlockSpec(memory_space=pltpu.SMEM),
            pl.BlockSpec((places, cores, 1, kinds, block, features), lambda p, h: (0, 0, p, 0, 0, 0)),
        ],
        out_specs=[
            pl.BlockSpec(
                (1, rows, rows),
                lambda p, h, part=part: (jnp.where(p < part, 0, jnp.where(p == part, h, heads - 1)), 0, 0),
            )
            for part in range(parts)
        ],
        out_shape=[pltpu.HBM((heads, rows, rows), jnp.bfloat16)] * parts,
        compiler_params=params(2),
    )(core.reshape(1), pair)


def mix_kernel(place, weights, *refs):
    pieces, (near, far, value, held, held_weights, arrived) = refs[:-6], refs[-6:]
    each, cores, rows, features = pieces[0].shape
    half = value.shape[0] // cores
    heads = features // HEAD_DIM
    copies = [
        pltpu.make_async_copy(piece, held.at[k], arrived.at[k]) for k, piece in enumerate(pieces)
    ]
    copies += [
        pltpu.make_async_copy(weights.at[head], held_weights.at[head], arrived.at[len(pieces) + head])
        for head in range(heads)
    ]
    for copy in copies:
        copy.start()
    for k in range(len(pieces)):
        copies[k].wait()
        for j in range(each):
            at = pl.multiple_of((place[0] ^ (k * each + j)) * rows, rows)
            for core in range(cores):
                value[pl.ds(core * half + at, rows), :] = held[k, j, core].astype(value.dtype)
    mixed = []
    for head in range(heads):
        copies[len(pieces) + head].wait()
        lanes = slice(head_start(head), head_start(head) + SPAN)
        mixed.append(
            jnp.dot(
                held_weights[head], value[:, lanes].astype(jnp.bfloat16),
                preferred_element_type=jnp.float32,
            )
        )
    joined = joined_heads(mixed).astype(jnp.bfloat16)
    near[...] = joined[:half]
    far[...] = joined[half:]


def index_mix(place, weights, pieces):
    heads, rows, _ = weights.shape
    features = pieces[0].shape[-1]
    result = pltpu.VMEM((rows // 2, features), jnp.bfloat16)
    held = jnp.float32 if pieces[0].shape[2] % EDGE else jnp.bfloat16
    far = pl.BlockSpec(memory_space=pltpu.HBM)
    return pl.pallas_call(
        mix_kernel,
        in_specs=[pl.BlockSpec(memory_space=pltpu.SMEM)] + [far] * (1 + len(pieces)),
        out_specs=[pl.BlockSpec(memory_space=pltpu.VMEM)] * 2,
        out_shape=[result, result],
        scratch_shapes=[
            pltpu.VMEM((rows, features), held),
            pltpu.VMEM((len(pieces),) + pieces[0].shape, jnp.bfloat16),
            pltpu.VMEM(weights.shape, jnp.bfloat16),
            pltpu.SemaphoreType.DMA((len(pieces) + heads,)),
        ],
        compiler_params=params(),
    )(
        place.reshape(1),
        *[pltpu.with_memory_space_constraint(value, pltpu.HBM) for value in [weights] + pieces],
    )


def project_kernel(places, inner, scalars, near, far, proj_weight, proj_bias, *refs):
    core, twist = scalars[0], scalars[1]
    half = near.shape[1]
    total = proj_bias[...]
    for held, place in ((near, core), (far, 1 - core)):
        rows = pl.ds(pl.multiple_of(place * half, half), half)
        total = total + jnp.dot(held[...], proj_weight[rows, :], preferred_element_type=jnp.float32)
    total = total.astype(jnp.bfloat16)
    if len(refs) == 1:
        refs[0][...] = total
        return
    *outs, turned = refs
    block = total.shape[0] // places
    for place in range(places):
        turned[place] = total[place * block : (place + 1) * block]
    for k in range(places):
        outs[k % inner][k // inner] = turned[twist ^ k]


def project(near, far, proj_weight, proj_bias, core, row, places, inner):
    rows, width = near.shape[0], proj_weight.shape[1]
    block = rows // places
    shapes = [pltpu.HBM((rows, width), jnp.bfloat16)]
    if inner:
        shapes = [jax.ShapeDtypeStruct((places // inner, block, width), jnp.bfloat16)] * inner
    return pl.pallas_call(
        functools.partial(project_kernel, places, inner),
        in_specs=[pl.BlockSpec(memory_space=pltpu.SMEM)]
        + [pl.BlockSpec(memory_space=pltpu.VMEM)] * 4,
        out_specs=[pl.BlockSpec(memory_space=pltpu.VMEM)] * len(shapes),
        out_shape=shapes,
        scratch_shapes=[pltpu.VMEM((places, block, width), jnp.bfloat16)] if inner else [],
        compiler_params=params(),
    )(jnp.stack([core, row]), near, far, proj_weight, proj_bias.reshape(1, -1))


def gate_kernel(*refs):
    del refs


def gated(value, earlier):
    anywhere = pl.BlockSpec(memory_space=pl.ANY)
    return pl.pallas_call(
        gate_kernel,
        in_specs=[anywhere] * (1 + len(earlier)),
        out_specs=anywhere,
        out_shape=pltpu.HBM(value.shape, value.dtype),
        input_output_aliases={0: 0},
    )(value, *earlier)


def column_kernel(core, *refs):
    *lines, out = refs
    at = 0
    for ref in lines:
        for place in range(ref.shape[0]):
            first = ref[place, 0].astype(jnp.float32)[:1]
            last = ref[place, ref.shape[1] - 1].astype(jnp.float32)[ref.shape[2] - 1 :]
            out[at : at + 1, :] = jnp.where(core[0] == 0, last, first)
            at += 1


def next_column(core, lines):
    total = sum(value.shape[0] for value in lines)
    return pl.pallas_call(
        column_kernel,
        in_specs=[pl.BlockSpec(memory_space=pltpu.SMEM)]
        + [pl.BlockSpec(memory_space=pltpu.VMEM)] * len(lines),
        out_specs=pl.BlockSpec(memory_space=pltpu.VMEM),
        out_shape=jax.ShapeDtypeStruct((total, lines[0].shape[-1]), jnp.float32),
        compiler_params=params(),
    )(core.reshape(1), *lines)


def line_of(line, rows):
    quarter = rows // 4
    if line < quarter:
        return 0, line
    if line < 3 * quarter:
        return 1, line - quarter
    return 0, line - 2 * quarter


def conv_kernel(
    rows, cols, count, scalars, *refs,
):
    core, twist = scalars[0], scalars[1]
    middles, refs = refs[:count], refs[count:]
    (
        outer, above, below, side_outer, side_middle, keep,
        first_kernel, first_bias, second_kernel, second_bias, out,
        taken, even, odd, acted, woven, middle, second_held, fetched,
    ) = refs
    fetches = [
        pltpu.make_async_copy(second_kernel, second_held, fetched.at[0]),
    ]
    for fetch in fetches:
        fetch.start()
    pitch = cols + EDGE
    depth = CHANNELS
    place = lax.broadcasted_iota(jnp.int32, (EDGE, 1), 0)
    half = 2 * depth
    _, windows, piece, _ = outer.shape
    per = TILE_COLS // piece
    if count > 1:
        each = middle.shape[0] // count
        for k in range(count):
            for j in range(each):
                middle[twist ^ (k * each + j)] = middles[k][j]
    else:
        middle[...] = middles[0][...]

    def side(token, lanes, first):
        within = 0 if first else per - 1
        if token == 0 or token == rows + 1:
            edge, at = side_outer, (0 if token == 0 else rows // 2 + 1)
        else:
            part, at = line_of(token - 1, rows)
            edge, at = (side_middle, at) if part else (side_outer, at + 1)
        at = at * per + within
        if edge is side_middle:
            found = edge[pl.ds(at ^ twist, 1), lanes]
        else:
            found = edge[at : at + 1, lanes]
        return jnp.where(core == (0 if first else 1), found, 0.0)

    def gap_of(row):
        block = jnp.zeros((EDGE, half), jnp.float32)
        if row >= 1:
            token, sub = (row - 1) // 2, (row - 1) % 2
            block = jnp.where(place == 0, side(token, slice(sub * half, (sub + 1) * half), True), block)
        if row < 2 * (rows + 2):
            token, sub = row // 2, row % 2
            block = jnp.where(
                place == EDGE - 1, side(token, slice(sub * half, (sub + 1) * half), False), block
            )
        return block

    taken[0:EDGE, 0:depth] = jnp.zeros((EDGE, depth), jnp.bfloat16)
    for i in range(rows + 2):
        if i == 0:
            source, at = above, 0
        elif i == rows + 1:
            source, at = below, 0
        else:
            part, at = line_of(i - 1, rows)
            source = (outer, middle)[part]
        body = jnp.concatenate(
            [
                source[at * per + across, window].astype(jnp.float32)
                for window in range(windows)
                for across in range(per)
            ],
            axis=0,
        )
        for p in range(2):
            lanes = slice(p * half, (p + 1) * half)
            y = 2 * i + p
            line = jnp.concatenate([gap_of(y), body[:, lanes], gap_of(y + 1)], axis=0)
            length = line.shape[0]
            base = y * pitch
            taken[base : base + length, depth : 3 * depth] = line.astype(jnp.bfloat16)
            later = pltpu.roll(line[:, depth:], 1, 0)
            sooner = pltpu.roll(line[:, :depth], length - 1, 0)
            taken[base + EDGE : base + length, 0:depth] = later[EDGE:].astype(jnp.bfloat16)
            taken[base : base + pitch, 3 * depth :] = sooner[:pitch].astype(jnp.bfloat16)
    last = 2 * (rows + 2) * pitch
    taken[last : last + EDGE, 3 * depth :] = jnp.zeros((EDGE, depth), jnp.bfloat16)

    lines = 2 * rows
    total = (lines + 2) * pitch + EDGE
    even[0:EDGE] = jnp.zeros((EDGE, depth), jnp.float32)
    odd[0:EDGE] = jnp.zeros((EDGE, depth), jnp.float32)
    even[EDGE + total :] = jnp.zeros((EDGE, depth), jnp.float32)
    odd[EDGE + total :] = jnp.zeros((EDGE, depth), jnp.float32)

    def taps(source, kernel, starts, size, q):
        found = None
        for r in range(3):
            cells = [
                source[at + r * pitch : at + r * pitch + size, q * depth : (q + 3) * depth]
                for at in starts
            ]
            cells = cells[0] if len(cells) == 1 else jnp.concatenate(cells, axis=0)
            part = jnp.dot(cells, kernel[r], preferred_element_type=jnp.float32)
            found = part if found is None else found + part
        return found

    step = -(-total // 6 // EDGE) * EDGE
    for at in range(0, total, step):
        size = min(step, total - at)
        kept = keep[at : at + size, :] > 0.0
        kept = jnp.concatenate([kept] * (depth // LANES), axis=1)
        for q, held in ((0, even), (1, odd)):
            value = taps(taken, first_kernel, [at], size, q) + first_bias[...]
            value = jax.nn.gelu(value)
            held[EDGE + at : EDGE + at + size] = jnp.where(kept, value, 0.0)
    acted[:, depth : 2 * depth] = even[EDGE : EDGE + total].astype(jnp.bfloat16)
    acted[:, 2 * depth : 3 * depth] = odd[EDGE : EDGE + total].astype(jnp.bfloat16)
    acted[:, 0:depth] = odd[EDGE - 1 : EDGE - 1 + total].astype(jnp.bfloat16)
    acted[:, 3 * depth :] = even[EDGE + 1 : EDGE + 1 + total].astype(jnp.bfloat16)

    fetches[0].wait()
    group = max(lines // 8, 1)
    for at in range(0, lines, group):
        for q in range(2):
            starts = [EDGE + (at + y) * pitch for y in range(group)]
            value = taps(acted, second_held, starts, cols, q) + second_bias[...]
            for y in range(group):
                for lane in range(depth // LANES):
                    woven[lane, pl.ds((at + y) * 2 * cols + q, cols, stride=2), :] = value[
                        y * cols : (y + 1) * cols, lane * LANES : (lane + 1) * LANES
                    ]
    for lane in range(depth // LANES):
        out[:, lane * LANES : (lane + 1) * LANES] = woven[lane].astype(jnp.bfloat16)


def convolve_twice(
    scalars, middles, outer, above, below, side_outer, side_middle, keep,
    first_kernel, first_bias, second_kernel, second_bias,
):
    places, windows, piece, width = outer.shape
    rows, cols = 2 * places * piece // TILE_COLS, windows * TILE_COLS
    pitch = cols + EDGE
    total = (2 * rows + 2) * pitch + EDGE
    depth = CHANNELS
    near = pl.BlockSpec(memory_space=pltpu.VMEM)
    far = pl.BlockSpec(memory_space=pltpu.HBM)
    kernels = [kernel.reshape(3, 3 * depth, depth) for kernel in (first_kernel, second_kernel)]
    kernels[1] = pltpu.with_memory_space_constraint(kernels[1], pltpu.HBM)
    found = pl.pallas_call(
        functools.partial(conv_kernel, rows, cols, len(middles)),
        out_shape=jax.ShapeDtypeStruct((4 * rows * cols, depth), jnp.bfloat16),
        in_specs=[pl.BlockSpec(memory_space=pltpu.SMEM)]
        + [near] * (len(middles) + 6)
        + [near, near, far, near],
        out_specs=near,
        scratch_shapes=[
            pltpu.VMEM(((2 * rows + 4) * pitch + EDGE, 4 * depth), jnp.bfloat16),
            pltpu.VMEM((total + 2 * EDGE, depth), jnp.float32),
            pltpu.VMEM((total + 2 * EDGE, depth), jnp.float32),
            pltpu.VMEM((total, 4 * depth), jnp.bfloat16),
            pltpu.VMEM((depth // LANES, 4 * rows * cols, LANES), jnp.float32),
            pltpu.VMEM(outer.shape, jnp.bfloat16),
            pltpu.VMEM((3, 3 * depth, depth), jnp.bfloat16),
            pltpu.SemaphoreType.DMA((1,)),
        ],
        compiler_params=params(size=2 * VMEM_BYTES),
    )(
        scalars, *middles, outer, above, below, side_outer, side_middle, keep,
        kernels[0], first_bias.reshape(1, depth), kernels[1], second_bias.reshape(1, depth),
    )
    return found.reshape(2 * rows, 2 * cols, depth)


def kept_rows(rows, cols):
    pitch = cols + EDGE
    lines = 2 * rows
    total = (lines + 2) * pitch + EDGE
    row, col = lax.axis_index("row"), lax.axis_index("col")
    top, bottom = row == 0, row == lax.axis_size("row") - 1
    start, end = col == 0, col == lax.axis_size("col") - 1
    flat = jnp.arange(total)
    line, place = flat // pitch - 1, flat % pitch - EDGE
    wrapped = place == -EDGE
    line = jnp.where(wrapped, line - 1, line)
    place = jnp.where(wrapped, cols, place)
    outside = (
        ((line < 0) & top) | ((line >= lines) & bottom)
        | ((place < 0) & start) | ((place >= cols) & end)
    )
    return jnp.broadcast_to(jnp.where(outside, 0.0, 1.0)[:, None], (total, LANES)).astype(jnp.float32)


def shifted(value, axis, by):
    size = lax.axis_size(axis)
    pairs = [(i, i + by) for i in range(size) if 0 <= i + by < size]
    return lax.ppermute(value, axis, pairs)


def swapped(value, axis, by):
    return lax.ppermute(value, axis, [(i, i ^ by) for i in range(lax.axis_size(axis))])


def exchanged(value, axes):
    return lax.all_to_all(value, axes, split_axis=0, concat_axis=0, tiled=True)


def in_pieces(value):
    places, windows, owned, width = value.shape
    if owned < PIECE:
        joined = value.reshape(-1, PIECE // owned, windows, owned, width)
        return jnp.swapaxes(joined, 1, 2).reshape(-1, windows, PIECE, width)
    cut = value.reshape(places, windows, owned // PIECE, PIECE, width)
    return jnp.swapaxes(cut, 1, 2).reshape(-1, windows, PIECE, width)


def picked(value, index, axis=0):
    return lax.dynamic_index_in_dim(value, index, axis, keepdims=False)


def after(value, *earlier):
    corners = tuple(array[(0,) * (array.ndim - 2)][:PIECE, :LANES] for array in earlier)
    return lax.optimization_barrier((value,) + corners)[0]


def shards(
    query_window, key_window, value_window, query_index, key_index,
    proj_weight, proj_bias, first_kernel, first_bias, second_kernel, second_bias,
):
    rows_dev, cols_dev, tokens_win, features = query_window.shape
    windows = rows_dev * cols_dev
    flat = (windows, tokens_win, features)
    inner, cores, places = 2, lax.axis_size("col"), lax.axis_size("row")
    outer = places // inner
    row, core = lax.axis_index("row"), lax.axis_index("col")
    z, y = row // inner, row % inner
    chunk = tokens_win // 2
    owned = chunk // places
    half = features // cores

    def slab_of(value, part, place, count):
        at = place * owned
        if part == 0:
            at = jnp.where(at < chunk // 2, at, at + chunk)
        else:
            at = at + chunk // 2
        cut = lax.dynamic_slice_in_dim(value, at, count * owned, axis=value.ndim - 2)
        return cut.reshape(cut.shape[:-2] + (count, owned, cut.shape[-1]))

    query, key_rows = query_index.reshape(flat), key_index.reshape(flat)
    pair = exchanged(
        dealt(query, key_rows, places, cores).reshape(places * cores, 2, 2, windows * owned, half),
        ("row", "col"),
    ).reshape(places, cores, 2, 2, windows * owned, half)

    window_out = window_attend(
        query_window.reshape(flat), key_window.reshape(flat),
        value_window.reshape(flat), cores,
    )
    window_out = jnp.stack([picked(window_out, core), swapped(picked(window_out, 1 - core), "col", 1)])
    blocks = jnp.stack(
        [
            jnp.stack([slab_of(window_out, part, (z ^ k) * inner, inner) for part in range(2)])
            for k in range(outer)
        ]
    )
    values_near, values_far = picked(blocks, y, 4), swapped(picked(blocks, 1 - y, 4), "row", 1)
    pieces = []
    for part in range(2):
        pieces.append([])
        for k in range(outer):
            piece = jnp.stack([values_near[k, part], values_far[k, part]])
            piece = piece.reshape(inner, cores, windows * owned, half)
            pieces[part].append(swapped(piece, "row", k * inner) if k else piece)
    weights = index_weights(core, pair, owned)
    keep = kept_rows(rows_dev * TILE_ROWS, cols_dev * TILE_COLS)

    images = []
    earlier = []
    line = TILE_COLS // PIECE

    def projected_of(part, apart):
        near, far = index_mix(row, weights[part], pieces[part])
        return project(
            near, swapped(far, "col", 1), proj_weight, proj_bias, core, row, places, apart
        )

    projected = gated(projected_of(0, 0)[0], pieces[1])
    outer_rows = in_pieces(exchanged(projected.reshape(places, windows, owned, -1), "row"))
    above = shifted(outer_rows[-line:], "row", 1)
    below = shifted(outer_rows[:line], "row", -1)
    side_outer = swapped(next_column(core, [above, outer_rows, below]), "col", 1)
    if owned == PIECE:
        middles = [
            (swapped(block, "row", k) if k else block).reshape(1, windows, owned, -1)
            for k, block in enumerate(projected_of(1, places))
        ]
        twist = row
    else:
        projected = projected_of(1, 0)[0].reshape(places, windows, owned, -1)
        middles = [in_pieces(exchanged(projected, "row"))]
        twist = jnp.zeros_like(row)
    side_middle = swapped(next_column(core, middles), "col", 1)
    return convolve_twice(
        jnp.stack([core, twist]), middles, outer_rows, above, below, side_outer, side_middle, keep,
        first_kernel, first_bias, second_kernel, second_bias,
    )


def solution(mesh):
    spread = P(("grp", "row"), "col", None, None)
    in_specs = (spread,) * 5 + (P(),) * 6
    out_specs = P(("grp", "row"), "col", None)
    return jax.shard_map(shards, mesh=mesh, in_specs=in_specs, out_specs=out_specs, check_vma=False)
```

```python
import functools
import math

import jax
import jax.numpy as jnp
from jax import lax
from jax.experimental import pallas as pl
from jax.experimental.pallas import tpu as pltpu
from jax.sharding import PartitionSpec as P

HEADS = 8
HEAD_DIM = 160
CHANNELS = 256
TILE_ROWS = 8
TILE_COLS = 16
LANES = 128
EDGE = 16
PIECE = 8
SPAN = 2 * LANES
VMEM_BYTES = 16 * 1024 * 1024


def params(steps=0, size=VMEM_BYTES):
    return pltpu.CompilerParams(
        dimension_semantics=("arbitrary",) * steps if steps else None,
        vmem_limit_bytes=size,
    )


def head_start(head):
    return head * HEAD_DIM // LANES * LANES


def head_mask(head):
    lane = lax.broadcasted_iota(jnp.int32, (1, SPAN), 1) + head_start(head)
    return (lane >= head * HEAD_DIM) & (lane < (head + 1) * HEAD_DIM)


def joined_heads(mixed):
    tiles = []
    lane = lax.broadcasted_iota(jnp.int32, (1, LANES), 1)
    for tile in range(len(mixed) * HEAD_DIM // LANES):
        base = tile * LANES
        first, last = base // HEAD_DIM, (base + LANES - 1) // HEAD_DIM
        pieces = []
        for head in (first, last):
            at = base - head_start(head)
            pieces.append(mixed[head][:, at : at + LANES])
        if first == last:
            tiles.append(pieces[0])
        else:
            tiles.append(jnp.where(lane < last * HEAD_DIM - base, pieces[0], pieces[1]))
    return jnp.concatenate(tiles, axis=1)


def softmax_rows(scores):
    raised = jnp.exp(scores - jnp.max(scores, axis=-1, keepdims=True))
    return (raised / jnp.sum(raised, axis=-1, keepdims=True)).astype(jnp.bfloat16)


def window_kernel(query, key_rows, value, out):
    mixed = []
    for head in range(HEADS):
        lanes = pl.ds(head_start(head), SPAN)
        masked = jnp.where(head_mask(head), query[0, :, lanes], 0)
        scores = lax.dot_general(
            masked, key_rows[0, :, lanes], (((1,), (1,)), ((), ())),
            preferred_element_type=jnp.float32,
        ) * (1.0 / math.sqrt(HEAD_DIM))
        mixed.append(
            jnp.dot(softmax_rows(scores), value[0, :, lanes], preferred_element_type=jnp.float32)
        )
    joined = joined_heads(mixed).astype(jnp.bfloat16)
    parts, features = out.shape[0], out.shape[-1]
    for part in range(parts):
        out[part, 0] = joined[:, part * features : (part + 1) * features]


def window_attend(query, key_rows, value, parts):
    windows, tokens, features = query.shape
    result = (parts, windows, tokens, features // parts)
    block = pl.BlockSpec((1, tokens, features), lambda w: (w, 0, 0))
    return pl.pallas_call(
        window_kernel,
        grid=(windows,),
        in_specs=[block] * 3,
        out_specs=pl.BlockSpec((parts, 1, tokens, features // parts), lambda w: (0, w, 0, 0)),
        out_shape=jax.ShapeDtypeStruct(result, jnp.bfloat16),
        compiler_params=params(1),
    )(query, key_rows, value)


def token_of(place, part, owned, places):
    chunk = owned * places
    if part:
        return chunk // 2 + place * owned
    return place * owned if place * owned < chunk // 2 else chunk + place * owned


def deal_kernel(query, key_rows, out, held, packed, arrived, left):
    places, cores, parts, kinds, block, half = out.shape
    windows = query.shape[0]
    owned = block // windows
    arriving = [
        pltpu.make_async_copy(source, held.at[kind], arrived.at[kind])
        for kind, source in enumerate((query, key_rows))
    ]
    for copy in arriving:
        copy.start()
    leaving = []
    for kind in range(kinds):
        arriving[kind].wait()
        for place in range(places):
            for part in range(parts):
                rows = pl.ds(token_of(place, part, owned, places), owned)
                for window in range(windows):
                    for core in range(cores):
                        packed[kind, place, core, part, pl.ds(window * owned, owned), :] = held[
                            kind, window, rows, core * half : (core + 1) * half
                        ]
        copy = pltpu.make_async_copy(packed.at[kind], out.at[:, :, :, kind], left.at[kind])
        copy.start()
        leaving.append(copy)
    for copy in leaving:
        copy.wait()


def dealt(query, key_rows, places, cores):
    windows, tokens, features = query.shape
    result = (places, cores, 2, 2, windows * tokens // (2 * places), features // cores)
    return pl.pallas_call(
        deal_kernel,
        in_specs=[pl.BlockSpec(memory_space=pltpu.HBM)] * 2,
        out_specs=pl.BlockSpec(memory_space=pltpu.HBM),
        out_shape=pltpu.HBM(result, query.dtype),
        scratch_shapes=[
            pltpu.VMEM((2,) + query.shape, query.dtype),
            pltpu.VMEM((2,) + result[:3] + result[4:], query.dtype),
            pltpu.SemaphoreType.DMA((2,)),
            pltpu.SemaphoreType.DMA((2,)),
        ],
        compiler_params=params(),
    )(
        pltpu.with_memory_space_constraint(query, pltpu.HBM),
        pltpu.with_memory_space_constraint(key_rows, pltpu.HBM),
    )


def weights_kernel(tokens, core, pair, *outs):
    places, cores, _, _, block, _ = pair.shape
    head = pl.program_id(1)
    start = head * HEAD_DIM // LANES * LANES
    lanes = pl.ds(pl.multiple_of(start, LANES), SPAN)
    lane = lax.broadcasted_iota(jnp.int32, (1, SPAN), 1) + start
    inside = (lane >= head * HEAD_DIM) & (lane < (head + 1) * HEAD_DIM)
    held = jnp.float32 if block % EDGE else jnp.bfloat16

    def gathered(kind):
        return jnp.concatenate(
            [
                pair[place, core[0] ^ far, 0, kind, :, lanes].astype(held)
                for far in range(cores)
                for place in range(places)
            ],
            axis=0,
        ).astype(jnp.bfloat16)

    scores = lax.dot_general(
        jnp.where(inside, gathered(0), 0), gathered(1), (((1,), (1,)), ((), ())),
        preferred_element_type=jnp.float32,
    ) * (1.0 / math.sqrt(HEAD_DIM))
    rows = scores.shape[0]
    token_row = lax.broadcasted_iota(jnp.int32, (rows, 1), 0) % tokens
    token_col = lax.broadcasted_iota(jnp.int32, (1, rows), 1) % tokens
    found = softmax_rows(jnp.where(token_row == token_col, scores, -jnp.inf))
    for part, out in enumerate(outs):

        @pl.when(pl.program_id(0) == part)
        def _(out=out):
            out[0] = found


def index_weights(core, pair, tokens):
    places, cores, parts, kinds, block, features = pair.shape
    heads = features // HEAD_DIM
    rows = places * cores * block
    return pl.pallas_call(
        functools.partial(weights_kernel, tokens),
        grid=(parts, heads),
        in_specs=[
            pl.BlockSpec(memory_space=pltpu.SMEM),
            pl.BlockSpec((places, cores, 1, kinds, block, features), lambda p, h: (0, 0, p, 0, 0, 0)),
        ],
        out_specs=[
            pl.BlockSpec(
                (1, rows, rows),
                lambda p, h, part=part: (jnp.where(p < part, 0, jnp.where(p == part, h, heads - 1)), 0, 0),
            )
            for part in range(parts)
        ],
        out_shape=[
            (pltpu.HBM if part else pltpu.VMEM)((heads, rows, rows), jnp.bfloat16) for part in range(parts)
        ],
        compiler_params=params(2),
    )(core.reshape(1), pair)


def mix_kernel(fetched, place, weights, *refs):
    pieces, (near, far, value, held, held_weights, arrived) = refs[:-6], refs[-6:]
    each, cores, rows, features = pieces[0].shape
    half = value.shape[0] // cores
    heads = features // HEAD_DIM
    copies = []
    if fetched:
        copies = [
            pltpu.make_async_copy(piece, held.at[k], arrived.at[k]) for k, piece in enumerate(pieces)
        ]
        copies += [
            pltpu.make_async_copy(weights.at[head], held_weights.at[head], arrived.at[len(pieces) + head])
            for head in range(heads)
        ]
    for copy in copies:
        copy.start()
    for k, piece in enumerate(pieces):
        if fetched:
            copies[k].wait()
            piece = held.at[k]
        for j in range(each):
            at = pl.multiple_of((place[0] ^ (k * each + j)) * rows, rows)
            for core in range(cores):
                value[pl.ds(core * half + at, rows), :] = piece[j, core].astype(value.dtype)
    mixed = []
    for head in range(heads):
        if fetched:
            copies[len(pieces) + head].wait()
        lanes = slice(head_start(head), head_start(head) + SPAN)
        mixed.append(
            jnp.dot(
                (held_weights if fetched else weights)[head], value[:, lanes].astype(jnp.bfloat16),
                preferred_element_type=jnp.float32,
            )
        )
    joined = joined_heads(mixed).astype(jnp.bfloat16)
    near[...] = joined[:half]
    far[...] = joined[half:]


def index_mix(place, weights, pieces, fetched):
    heads, rows, _ = weights.shape
    features = pieces[0].shape[-1]
    result = pltpu.VMEM((rows // 2, features), jnp.bfloat16)
    held = jnp.float32 if pieces[0].shape[2] % EDGE else jnp.bfloat16
    source = pl.BlockSpec(memory_space=pltpu.HBM if fetched else pltpu.VMEM)
    if fetched:
        weights, *pieces = [
            pltpu.with_memory_space_constraint(value, pltpu.HBM) for value in [weights] + pieces
        ]
    return pl.pallas_call(
        functools.partial(mix_kernel, fetched),
        in_specs=[pl.BlockSpec(memory_space=pltpu.SMEM)] + [source] * (1 + len(pieces)),
        out_specs=[pl.BlockSpec(memory_space=pltpu.VMEM)] * 2,
        out_shape=[result, result],
        scratch_shapes=[
            pltpu.VMEM((rows, features), held),
            pltpu.VMEM((len(pieces),) + pieces[0].shape, jnp.bfloat16),
            pltpu.VMEM(weights.shape if fetched else (1, EDGE, LANES), jnp.bfloat16),
            pltpu.SemaphoreType.DMA((len(pieces) + heads,)),
        ],
        compiler_params=params(),
    )(
        place.reshape(1), weights, *pieces,
    )


def project_kernel(places, inner, scalars, near, far, proj_weight, proj_bias, *refs):
    core, twist = scalars[0], scalars[1]
    half = near.shape[1]
    total = proj_bias[...]
    for held, place in ((near, core), (far, 1 - core)):
        rows = pl.ds(pl.multiple_of(place * half, half), half)
        total = total + jnp.dot(held[...], proj_weight[rows, :], preferred_element_type=jnp.float32)
    total = total.astype(jnp.bfloat16)
    if len(refs) == 1:
        refs[0][...] = total
        return
    *outs, turned = refs
    block = total.shape[0] // places
    for place in range(places):
        turned[place] = total[place * block : (place + 1) * block]
    for k in range(places):
        outs[k % inner][k // inner] = turned[twist ^ k]


def project(near, far, proj_weight, proj_bias, core, row, places, inner):
    rows, width = near.shape[0], proj_weight.shape[1]
    block = rows // places
    shapes = [pltpu.HBM((rows, width), jnp.bfloat16)]
    if inner:
        shapes = [jax.ShapeDtypeStruct((places // inner, block, width), jnp.bfloat16)] * inner
    return pl.pallas_call(
        functools.partial(project_kernel, places, inner),
        in_specs=[pl.BlockSpec(memory_space=pltpu.SMEM)]
        + [pl.BlockSpec(memory_space=pltpu.VMEM)] * 4,
        out_specs=[pl.BlockSpec(memory_space=pltpu.VMEM)] * len(shapes),
        out_shape=shapes,
        scratch_shapes=[pltpu.VMEM((places, block, width), jnp.bfloat16)] if inner else [],
        compiler_params=params(),
    )(jnp.stack([core, row]), near, far, proj_weight, proj_bias.reshape(1, -1))


def gate_kernel(*refs):
    del refs


def gated(value, earlier):
    anywhere = pl.BlockSpec(memory_space=pl.ANY)
    return pl.pallas_call(
        gate_kernel,
        in_specs=[anywhere] * (1 + len(earlier)),
        out_specs=anywhere,
        out_shape=pltpu.HBM(value.shape, value.dtype),
        input_output_aliases={0: 0},
    )(value, *earlier)


def column_kernel(core, *refs):
    *lines, out = refs
    at = 0
    for ref in lines:
        for place in range(ref.shape[0]):
            first = ref[place, 0].astype(jnp.float32)[:1]
            last = ref[place, ref.shape[1] - 1].astype(jnp.float32)[ref.shape[2] - 1 :]
            out[at : at + 1, :] = jnp.where(core[0] == 0, last, first)
            at += 1


def next_column(core, lines):
    total = sum(value.shape[0] for value in lines)
    return pl.pallas_call(
        column_kernel,
        in_specs=[pl.BlockSpec(memory_space=pltpu.SMEM)]
        + [pl.BlockSpec(memory_space=pltpu.VMEM)] * len(lines),
        out_specs=pl.BlockSpec(memory_space=pltpu.VMEM),
        out_shape=jax.ShapeDtypeStruct((total, lines[0].shape[-1]), jnp.float32),
        compiler_params=params(),
    )(core.reshape(1), *lines)


def line_of(line, rows):
    quarter = rows // 4
    if line < quarter:
        return 0, line
    if line < 3 * quarter:
        return 1, line - quarter
    return 0, line - 2 * quarter


def conv_kernel(
    rows, cols, count, scalars, *refs,
):
    core, twist = scalars[0], scalars[1]
    middles, refs = refs[:count], refs[count:]
    (
        outer, above, below, side_outer, side_middle, keep,
        first_kernel, first_bias, second_kernel, second_bias, out,
        taken, even, odd, acted, woven, middle, second_held, fetched, ready, left,
    ) = refs
    fetches = [
        pltpu.make_async_copy(second_kernel, second_held, fetched.at[0]),
    ]
    for fetch in fetches:
        fetch.start()
    pitch = cols + EDGE
    depth = CHANNELS
    place = lax.broadcasted_iota(jnp.int32, (EDGE, 1), 0)
    half = 2 * depth
    _, windows, piece, _ = outer.shape
    per = TILE_COLS // piece
    if count > 1:
        each = middle.shape[0] // count
        for k in range(count):
            for j in range(each):
                middle[twist ^ (k * each + j)] = middles[k][j]
    else:
        middle[...] = middles[0][...]

    def side(token, lanes, first):
        within = 0 if first else per - 1
        if token == 0 or token == rows + 1:
            edge, at = side_outer, (0 if token == 0 else rows // 2 + 1)
        else:
            part, at = line_of(token - 1, rows)
            edge, at = (side_middle, at) if part else (side_outer, at + 1)
        at = at * per + within
        if edge is side_middle:
            found = edge[pl.ds(at ^ twist, 1), lanes]
        else:
            found = edge[at : at + 1, lanes]
        return jnp.where(core == (0 if first else 1), found, 0.0)

    def gap_of(row):
        block = jnp.zeros((EDGE, half), jnp.float32)
        if row >= 1:
            token, sub = (row - 1) // 2, (row - 1) % 2
            block = jnp.where(place == 0, side(token, slice(sub * half, (sub + 1) * half), True), block)
        if row < 2 * (rows + 2):
            token, sub = row // 2, row % 2
            block = jnp.where(
                place == EDGE - 1, side(token, slice(sub * half, (sub + 1) * half), False), block
            )
        return block

    taken[0:EDGE, 0:depth] = jnp.zeros((EDGE, depth), jnp.bfloat16)
    for i in range(rows + 2):
        if i == 0:
            source, at = above, 0
        elif i == rows + 1:
            source, at = below, 0
        else:
            part, at = line_of(i - 1, rows)
            source = (outer, middle)[part]
        body = jnp.concatenate(
            [
                source[at * per + across, window].astype(jnp.float32)
                for window in range(windows)
                for across in range(per)
            ],
            axis=0,
        )
        for p in range(2):
            lanes = slice(p * half, (p + 1) * half)
            y = 2 * i + p
            line = jnp.concatenate([gap_of(y), body[:, lanes], gap_of(y + 1)], axis=0)
            length = line.shape[0]
            base = y * pitch
            taken[base : base + length, depth : 3 * depth] = line.astype(jnp.bfloat16)
            later = pltpu.roll(line[:, depth:], 1, 0)
            sooner = pltpu.roll(line[:, :depth], length - 1, 0)
            taken[base + EDGE : base + length, 0:depth] = later[EDGE:].astype(jnp.bfloat16)
            taken[base : base + pitch, 3 * depth :] = sooner[:pitch].astype(jnp.bfloat16)
    last = 2 * (rows + 2) * pitch
    taken[last : last + EDGE, 3 * depth :] = jnp.zeros((EDGE, depth), jnp.bfloat16)

    lines = 2 * rows
    total = (lines + 2) * pitch + EDGE
    even[0:EDGE] = jnp.zeros((EDGE, depth), jnp.float32)
    odd[0:EDGE] = jnp.zeros((EDGE, depth), jnp.float32)
    even[EDGE + total :] = jnp.zeros((EDGE, depth), jnp.float32)
    odd[EDGE + total :] = jnp.zeros((EDGE, depth), jnp.float32)

    def taps(source, kernel, starts, size, q):
        found = None
        for r in range(3):
            cells = [
                source[at + r * pitch : at + r * pitch + size, q * depth : (q + 3) * depth]
                for at in starts
            ]
            cells = cells[0] if len(cells) == 1 else jnp.concatenate(cells, axis=0)
            part = jnp.dot(cells, kernel[r], preferred_element_type=jnp.float32)
            found = part if found is None else found + part
        return found

    step = -(-total // 6 // EDGE) * EDGE
    for at in range(0, total, step):
        size = min(step, total - at)
        kept = keep[at : at + size, :] > 0.0
        kept = jnp.concatenate([kept] * (depth // LANES), axis=1)
        for q, held in ((0, even), (1, odd)):
            value = taps(taken, first_kernel, [at], size, q) + first_bias[...]
            value = jax.nn.gelu(value)
            held[EDGE + at : EDGE + at + size] = jnp.where(kept, value, 0.0)
    acted[:, depth : 2 * depth] = even[EDGE : EDGE + total].astype(jnp.bfloat16)
    acted[:, 2 * depth : 3 * depth] = odd[EDGE : EDGE + total].astype(jnp.bfloat16)
    acted[:, 0:depth] = odd[EDGE - 1 : EDGE - 1 + total].astype(jnp.bfloat16)
    acted[:, 3 * depth :] = even[EDGE + 1 : EDGE + 1 + total].astype(jnp.bfloat16)

    fetches[0].wait()
    group = max(lines // 8, 1)
    leaving = []
    for at in range(0, lines, group):
        for q in range(2):
            starts = [EDGE + (at + y) * pitch for y in range(group)]
            value = taps(acted, second_held, starts, cols, q) + second_bias[...]
            for y in range(group):
                for lane in range(depth // LANES):
                    woven[lane, pl.ds((at + y) * 2 * cols + q, cols, stride=2), :] = value[
                        y * cols : (y + 1) * cols, lane * LANES : (lane + 1) * LANES
                    ]
        rows_here = pl.ds(at * 2 * cols, group * 2 * cols)
        for lane in range(depth // LANES):
            ready[rows_here, lane * LANES : (lane + 1) * LANES] = woven[lane, rows_here, :].astype(
                jnp.bfloat16
            )
        copy = pltpu.make_async_copy(ready.at[rows_here], out.at[rows_here], left.at[at // group])
        copy.start()
        leaving.append(copy)
    for copy in leaving:
        copy.wait()


def convolve_twice(
    scalars, middles, outer, above, below, side_outer, side_middle, keep,
    first_kernel, first_bias, second_kernel, second_bias,
):
    places, windows, piece, width = outer.shape
    rows, cols = 2 * places * piece // TILE_COLS, windows * TILE_COLS
    pitch = cols + EDGE
    total = (2 * rows + 2) * pitch + EDGE
    depth = CHANNELS
    near = pl.BlockSpec(memory_space=pltpu.VMEM)
    far = pl.BlockSpec(memory_space=pltpu.HBM)
    kernels = [kernel.reshape(3, 3 * depth, depth) for kernel in (first_kernel, second_kernel)]
    kernels[1] = pltpu.with_memory_space_constraint(kernels[1], pltpu.HBM)
    found = pl.pallas_call(
        functools.partial(conv_kernel, rows, cols, len(middles)),
        out_shape=pltpu.HBM((4 * rows * cols, depth), jnp.bfloat16),
        in_specs=[pl.BlockSpec(memory_space=pltpu.SMEM)]
        + [near] * (len(middles) + 6)
        + [near, near, far, near],
        out_specs=far,
        scratch_shapes=[
            pltpu.VMEM(((2 * rows + 4) * pitch + EDGE, 4 * depth), jnp.bfloat16),
            pltpu.VMEM((total + 2 * EDGE, depth), jnp.float32),
            pltpu.VMEM((total + 2 * EDGE, depth), jnp.float32),
            pltpu.VMEM((total, 4 * depth), jnp.bfloat16),
            pltpu.VMEM((depth // LANES, 4 * rows * cols, LANES), jnp.float32),
            pltpu.VMEM(outer.shape, jnp.bfloat16),
            pltpu.VMEM((3, 3 * depth, depth), jnp.bfloat16),
            pltpu.SemaphoreType.DMA((1,)),
            pltpu.VMEM((4 * rows * cols, depth), jnp.bfloat16),
            pltpu.SemaphoreType.DMA((2 * rows,)),
        ],
        compiler_params=params(size=2 * VMEM_BYTES),
    )(
        scalars, *middles, outer, above, below, side_outer, side_middle, keep,
        kernels[0], first_bias.reshape(1, depth), kernels[1], second_bias.reshape(1, depth),
    )
    return found.reshape(2 * rows, 2 * cols, depth)


def kept_rows(rows, cols):
    pitch = cols + EDGE
    lines = 2 * rows
    total = (lines + 2) * pitch + EDGE
    row, col = lax.axis_index("row"), lax.axis_index("col")
    top, bottom = row == 0, row == lax.axis_size("row") - 1
    start, end = col == 0, col == lax.axis_size("col") - 1
    flat = jnp.arange(total)
    line, place = flat // pitch - 1, flat % pitch - EDGE
    wrapped = place == -EDGE
    line = jnp.where(wrapped, line - 1, line)
    place = jnp.where(wrapped, cols, place)
    outside = (
        ((line < 0) & top) | ((line >= lines) & bottom)
        | ((place < 0) & start) | ((place >= cols) & end)
    )
    return jnp.broadcast_to(jnp.where(outside, 0.0, 1.0)[:, None], (total, LANES)).astype(jnp.float32)


def shifted(value, axis, by):
    size = lax.axis_size(axis)
    pairs = [(i, i + by) for i in range(size) if 0 <= i + by < size]
    return lax.ppermute(value, axis, pairs)


def swapped(value, axis, by):
    return lax.ppermute(value, axis, [(i, i ^ by) for i in range(lax.axis_size(axis))])


def exchanged(value, axes):
    return lax.all_to_all(value, axes, split_axis=0, concat_axis=0, tiled=True)


def in_pieces(value):
    places, windows, owned, width = value.shape
    if owned < PIECE:
        joined = value.reshape(-1, PIECE // owned, windows, owned, width)
        return jnp.swapaxes(joined, 1, 2).reshape(-1, windows, PIECE, width)
    cut = value.reshape(places, windows, owned // PIECE, PIECE, width)
    return jnp.swapaxes(cut, 1, 2).reshape(-1, windows, PIECE, width)


def picked(value, index, axis=0):
    return lax.dynamic_index_in_dim(value, index, axis, keepdims=False)


def after(value, *earlier):
    corners = tuple(array[(0,) * (array.ndim - 2)][:PIECE, :LANES] for array in earlier)
    return lax.optimization_barrier((value,) + corners)[0]


def shards(
    query_window, key_window, value_window, query_index, key_index,
    proj_weight, proj_bias, first_kernel, first_bias, second_kernel, second_bias,
):
    rows_dev, cols_dev, tokens_win, features = query_window.shape
    windows = rows_dev * cols_dev
    flat = (windows, tokens_win, features)
    inner, cores, places = 2, lax.axis_size("col"), lax.axis_size("row")
    outer = places // inner
    row, core = lax.axis_index("row"), lax.axis_index("col")
    z, y = row // inner, row % inner
    chunk = tokens_win // 2
    owned = chunk // places
    half = features // cores

    def slab_of(value, part, place, count):
        at = place * owned
        if part == 0:
            at = jnp.where(at < chunk // 2, at, at + chunk)
        else:
            at = at + chunk // 2
        cut = lax.dynamic_slice_in_dim(value, at, count * owned, axis=value.ndim - 2)
        return cut.reshape(cut.shape[:-2] + (count, owned, cut.shape[-1]))

    query, key_rows = query_index.reshape(flat), key_index.reshape(flat)
    pair = exchanged(
        dealt(query, key_rows, places, cores).reshape(places * cores, 2, 2, windows * owned, half),
        ("row", "col"),
    ).reshape(places, cores, 2, 2, windows * owned, half)

    window_out = window_attend(
        query_window.reshape(flat), key_window.reshape(flat),
        value_window.reshape(flat), cores,
    )
    window_out = jnp.stack([picked(window_out, core), swapped(picked(window_out, 1 - core), "col", 1)])
    blocks = jnp.stack(
        [
            jnp.stack([slab_of(window_out, part, (z ^ k) * inner, inner) for part in range(2)])
            for k in range(outer)
        ]
    )
    values_near, values_far = picked(blocks, y, 4), swapped(picked(blocks, 1 - y, 4), "row", 1)
    pieces = []
    for part in range(2):
        pieces.append([])
        for k in range(outer):
            piece = jnp.stack([values_near[k, part], values_far[k, part]])
            piece = piece.reshape(inner, cores, windows * owned, half)
            pieces[part].append(swapped(piece, "row", k * inner) if k else piece)
    weights = index_weights(core, pair, owned)
    keep = kept_rows(rows_dev * TILE_ROWS, cols_dev * TILE_COLS)

    images = []
    earlier = []
    line = TILE_COLS // PIECE

    def projected_of(part, apart):
        near, far = index_mix(row, weights[part], pieces[part], part > 0)
        return project(
            near, swapped(far, "col", 1), proj_weight, proj_bias, core, row, places, apart
        )

    projected = gated(projected_of(0, 0)[0], pieces[1])
    outer_rows = in_pieces(exchanged(projected.reshape(places, windows, owned, -1), "row"))
    above = shifted(outer_rows[-line:], "row", 1)
    below = shifted(outer_rows[:line], "row", -1)
    side_outer = swapped(next_column(core, [above, outer_rows, below]), "col", 1)
    if owned == PIECE:
        middles = [
            (swapped(block, "row", k) if k else block).reshape(1, windows, owned, -1)
            for k, block in enumerate(projected_of(1, places))
        ]
        twist = row
    else:
        projected = projected_of(1, 0)[0].reshape(places, windows, owned, -1)
        middles = [in_pieces(exchanged(projected, "row"))]
        twist = jnp.zeros_like(row)
    side_middle = swapped(next_column(core, middles), "col", 1)
    return convolve_twice(
        jnp.stack([core, twist]), middles, outer_rows, above, below, side_outer, side_middle, keep,
        first_kernel, first_bias, second_kernel, second_bias,
    )


def solution(mesh):
    spread = P(("grp", "row"), "col", None, None)
    in_specs = (spread,) * 5 + (P(),) * 6
    out_specs = P(("grp", "row"), "col", None)
    return jax.shard_map(shards, mesh=mesh, in_specs=in_specs, out_specs=out_specs, check_vma=False)
```

```python
import functools
import math

import jax
import jax.numpy as jnp
from jax import lax
from jax.experimental import pallas as pl
from jax.experimental.pallas import tpu as pltpu
from jax.sharding import PartitionSpec as P

HEADS = 8
HEAD_DIM = 160
CHANNELS = 256
TILE_ROWS = 8
TILE_COLS = 16
LANES = 128
EDGE = 16
PIECE = 8
SPAN = 2 * LANES
VMEM_BYTES = 16 * 1024 * 1024


def params(steps=0, size=VMEM_BYTES):
    return pltpu.CompilerParams(
        dimension_semantics=("arbitrary",) * steps if steps else None,
        vmem_limit_bytes=size,
    )


def head_start(head):
    return head * HEAD_DIM // LANES * LANES


def head_mask(head):
    lane = lax.broadcasted_iota(jnp.int32, (1, SPAN), 1) + head_start(head)
    return (lane >= head * HEAD_DIM) & (lane < (head + 1) * HEAD_DIM)


def joined_heads(mixed):
    tiles = []
    lane = lax.broadcasted_iota(jnp.int32, (1, LANES), 1)
    for tile in range(len(mixed) * HEAD_DIM // LANES):
        base = tile * LANES
        first, last = base // HEAD_DIM, (base + LANES - 1) // HEAD_DIM
        pieces = []
        for head in (first, last):
            at = base - head_start(head)
            pieces.append(mixed[head][:, at : at + LANES])
        if first == last:
            tiles.append(pieces[0])
        else:
            tiles.append(jnp.where(lane < last * HEAD_DIM - base, pieces[0], pieces[1]))
    return jnp.concatenate(tiles, axis=1)


def softmax_rows(scores):
    raised = jnp.exp(scores - jnp.max(scores, axis=-1, keepdims=True))
    return (raised / jnp.sum(raised, axis=-1, keepdims=True)).astype(jnp.bfloat16)


def window_kernel(query, key_rows, value, out):
    mixed = []
    for head in range(HEADS):
        lanes = pl.ds(head_start(head), SPAN)
        masked = jnp.where(head_mask(head), query[0, :, lanes], 0)
        scores = lax.dot_general(
            masked, key_rows[0, :, lanes], (((1,), (1,)), ((), ())),
            preferred_element_type=jnp.float32,
        ) * (1.0 / math.sqrt(HEAD_DIM))
        mixed.append(
            jnp.dot(softmax_rows(scores), value[0, :, lanes], preferred_element_type=jnp.float32)
        )
    joined = joined_heads(mixed).astype(jnp.bfloat16)
    parts, features = out.shape[0], out.shape[-1]
    for part in range(parts):
        out[part, 0] = joined[:, part * features : (part + 1) * features]


def window_attend(query, key_rows, value, parts):
    windows, tokens, features = query.shape
    result = (parts, windows, tokens, features // parts)
    block = pl.BlockSpec((1, tokens, features), lambda w: (w, 0, 0))
    return pl.pallas_call(
        window_kernel,
        grid=(windows,),
        in_specs=[block] * 3,
        out_specs=pl.BlockSpec((parts, 1, tokens, features // parts), lambda w: (0, w, 0, 0)),
        out_shape=jax.ShapeDtypeStruct(result, jnp.bfloat16),
        compiler_params=params(1),
    )(query, key_rows, value)


def token_of(place, part, owned, places):
    chunk = owned * places
    if part:
        return chunk // 2 + place * owned
    return place * owned if place * owned < chunk // 2 else chunk + place * owned


def deal_kernel(query, key_rows, out, held, packed, arrived, left):
    places, cores, parts, kinds, block, half = out.shape
    windows = query.shape[0]
    owned = block // windows
    arriving = [
        pltpu.make_async_copy(source, held.at[kind], arrived.at[kind])
        for kind, source in enumerate((query, key_rows))
    ]
    for copy in arriving:
        copy.start()
    leaving = []
    for kind in range(kinds):
        arriving[kind].wait()
        for place in range(places):
            for part in range(parts):
                rows = pl.ds(token_of(place, part, owned, places), owned)
                for window in range(windows):
                    for core in range(cores):
                        packed[kind, place, core, part, pl.ds(window * owned, owned), :] = held[
                            kind, window, rows, core * half : (core + 1) * half
                        ]
        copy = pltpu.make_async_copy(packed.at[kind], out.at[:, :, :, kind], left.at[kind])
        copy.start()
        leaving.append(copy)
    for copy in leaving:
        copy.wait()


def dealt(query, key_rows, places, cores):
    windows, tokens, features = query.shape
    result = (places, cores, 2, 2, windows * tokens // (2 * places), features // cores)
    return pl.pallas_call(
        deal_kernel,
        in_specs=[pl.BlockSpec(memory_space=pltpu.HBM)] * 2,
        out_specs=pl.BlockSpec(memory_space=pltpu.HBM),
        out_shape=pltpu.HBM(result, query.dtype),
        scratch_shapes=[
            pltpu.VMEM((2,) + query.shape, query.dtype),
            pltpu.VMEM((2,) + result[:3] + result[4:], query.dtype),
            pltpu.SemaphoreType.DMA((2,)),
            pltpu.SemaphoreType.DMA((2,)),
        ],
        compiler_params=params(),
    )(
        pltpu.with_memory_space_constraint(query, pltpu.HBM),
        pltpu.with_memory_space_constraint(key_rows, pltpu.HBM),
    )


def weights_kernel(tokens, core, pair, *outs):
    places, cores, _, _, block, _ = pair.shape
    head = pl.program_id(1)
    start = head * HEAD_DIM // LANES * LANES
    lanes = pl.ds(pl.multiple_of(start, LANES), SPAN)
    lane = lax.broadcasted_iota(jnp.int32, (1, SPAN), 1) + start
    inside = (lane >= head * HEAD_DIM) & (lane < (head + 1) * HEAD_DIM)
    held = jnp.float32 if block % EDGE else jnp.bfloat16

    def gathered(kind):
        return jnp.concatenate(
            [
                pair[place, core[0] ^ far, 0, kind, :, lanes].astype(held)
                for far in range(cores)
                for place in range(places)
            ],
            axis=0,
        ).astype(jnp.bfloat16)

    scores = lax.dot_general(
        jnp.where(inside, gathered(0), 0), gathered(1), (((1,), (1,)), ((), ())),
        preferred_element_type=jnp.float32,
    ) * (1.0 / math.sqrt(HEAD_DIM))
    rows = scores.shape[0]
    token_row = lax.broadcasted_iota(jnp.int32, (rows, 1), 0) % tokens
    token_col = lax.broadcasted_iota(jnp.int32, (1, rows), 1) % tokens
    found = softmax_rows(jnp.where(token_row == token_col, scores, -jnp.inf))
    for part, out in enumerate(outs):

        @pl.when(pl.program_id(0) == part)
        def _(out=out):
            out[0] = found


def index_weights(core, pair, tokens):
    places, cores, parts, kinds, block, features = pair.shape
    heads = features // HEAD_DIM
    rows = places * cores * block
    return pl.pallas_call(
        functools.partial(weights_kernel, tokens),
        grid=(parts, heads),
        in_specs=[
            pl.BlockSpec(memory_space=pltpu.SMEM),
            pl.BlockSpec((places, cores, 1, kinds, block, features), lambda p, h: (0, 0, p, 0, 0, 0)),
        ],
        out_specs=[
            pl.BlockSpec(
                (1, rows, rows),
                lambda p, h, part=part: (jnp.where(p < part, 0, jnp.where(p == part, h, heads - 1)), 0, 0),
            )
            for part in range(parts)
        ],
        out_shape=[
            pltpu.VMEM((heads, rows, rows), jnp.bfloat16) for part in range(parts)
        ],
        compiler_params=params(2),
    )(core.reshape(1), pair)


def mix_kernel(fetched, place, weights, *refs):
    pieces, (near, far, value, held, arrived) = refs[:-5], refs[-5:]
    each, cores, rows, features = pieces[0].shape
    half = value.shape[0] // cores
    heads = features // HEAD_DIM
    copies = []
    if fetched:
        copies = [
            pltpu.make_async_copy(piece, held.at[k], arrived.at[k]) for k, piece in enumerate(pieces)
        ]
    for copy in copies:
        copy.start()
    for k, piece in enumerate(pieces):
        if fetched:
            copies[k].wait()
            piece = held.at[k]
        for j in range(each):
            at = pl.multiple_of((place[0] ^ (k * each + j)) * rows, rows)
            for core in range(cores):
                value[pl.ds(core * half + at, rows), :] = piece[j, core].astype(value.dtype)
    mixed = []
    for head in range(heads):
        lanes = slice(head_start(head), head_start(head) + SPAN)
        mixed.append(
            jnp.dot(
                weights[head], value[:, lanes].astype(jnp.bfloat16),
                preferred_element_type=jnp.float32,
            )
        )
    joined = joined_heads(mixed).astype(jnp.bfloat16)
    near[...] = joined[:half]
    far[...] = joined[half:]


def index_mix(place, weights, pieces, fetched):
    heads, rows, _ = weights.shape
    features = pieces[0].shape[-1]
    result = pltpu.VMEM((rows // 2, features), jnp.bfloat16)
    held = jnp.float32 if pieces[0].shape[2] % EDGE else jnp.bfloat16
    source = pl.BlockSpec(memory_space=pltpu.HBM if fetched else pltpu.VMEM)
    if fetched:
        pieces = [pltpu.with_memory_space_constraint(piece, pltpu.HBM) for piece in pieces]
    return pl.pallas_call(
        functools.partial(mix_kernel, fetched),
        in_specs=[pl.BlockSpec(memory_space=pltpu.SMEM), pl.BlockSpec(memory_space=pltpu.VMEM)]
        + [source] * len(pieces),
        out_specs=[pl.BlockSpec(memory_space=pltpu.VMEM)] * 2,
        out_shape=[result, result],
        scratch_shapes=[
            pltpu.VMEM((rows, features), held),
            pltpu.VMEM((len(pieces),) + pieces[0].shape, jnp.bfloat16),
            pltpu.SemaphoreType.DMA((len(pieces),)),
        ],
        compiler_params=params(),
    )(
        place.reshape(1), weights, *pieces,
    )


def project_kernel(places, inner, scalars, near, far, proj_weight, proj_bias, *refs):
    core, twist = scalars[0], scalars[1]
    half = near.shape[1]
    total = proj_bias[...]
    for held, place in ((near, core), (far, 1 - core)):
        rows = pl.ds(pl.multiple_of(place * half, half), half)
        total = total + jnp.dot(held[...], proj_weight[rows, :], preferred_element_type=jnp.float32)
    total = total.astype(jnp.bfloat16)
    if len(refs) == 1:
        refs[0][...] = total
        return
    *outs, turned = refs
    block = total.shape[0] // places
    for place in range(places):
        turned[place] = total[place * block : (place + 1) * block]
    for k in range(places):
        outs[k % inner][k // inner] = turned[twist ^ k]


def project(near, far, proj_weight, proj_bias, core, row, places, inner):
    rows, width = near.shape[0], proj_weight.shape[1]
    block = rows // places
    shapes = [pltpu.HBM((rows, width), jnp.bfloat16)]
    if inner:
        shapes = [jax.ShapeDtypeStruct((places // inner, block, width), jnp.bfloat16)] * inner
    return pl.pallas_call(
        functools.partial(project_kernel, places, inner),
        in_specs=[pl.BlockSpec(memory_space=pltpu.SMEM)]
        + [pl.BlockSpec(memory_space=pltpu.VMEM)] * 4,
        out_specs=[pl.BlockSpec(memory_space=pltpu.VMEM)] * len(shapes),
        out_shape=shapes,
        scratch_shapes=[pltpu.VMEM((places, block, width), jnp.bfloat16)] if inner else [],
        compiler_params=params(),
    )(jnp.stack([core, row]), near, far, proj_weight, proj_bias.reshape(1, -1))


def gate_kernel(*refs):
    del refs


def gated(value, earlier):
    anywhere = pl.BlockSpec(memory_space=pl.ANY)
    return pl.pallas_call(
        gate_kernel,
        in_specs=[anywhere] * (1 + len(earlier)),
        out_specs=anywhere,
        out_shape=pltpu.HBM(value.shape, value.dtype),
        input_output_aliases={0: 0},
    )(value, *earlier)


def column_kernel(core, *refs):
    *lines, out = refs
    at = 0
    for ref in lines:
        for place in range(ref.shape[0]):
            first = ref[place, 0].astype(jnp.float32)[:1]
            last = ref[place, ref.shape[1] - 1].astype(jnp.float32)[ref.shape[2] - 1 :]
            out[at : at + 1, :] = jnp.where(core[0] == 0, last, first)
            at += 1


def next_column(core, lines):
    total = sum(value.shape[0] for value in lines)
    return pl.pallas_call(
        column_kernel,
        in_specs=[pl.BlockSpec(memory_space=pltpu.SMEM)]
        + [pl.BlockSpec(memory_space=pltpu.VMEM)] * len(lines),
        out_specs=pl.BlockSpec(memory_space=pltpu.VMEM),
        out_shape=jax.ShapeDtypeStruct((total, lines[0].shape[-1]), jnp.float32),
        compiler_params=params(),
    )(core.reshape(1), *lines)


def line_of(line, rows):
    quarter = rows // 4
    if line < quarter:
        return 0, line
    if line < 3 * quarter:
        return 1, line - quarter
    return 0, line - 2 * quarter


def conv_kernel(
    rows, cols, count, scalars, *refs,
):
    core, twist = scalars[0], scalars[1]
    middles, refs = refs[:count], refs[count:]
    (
        outer, above, below, side_outer, side_middle, keep,
        first_kernel, first_bias, second_kernel, second_bias, out,
        taken, even, odd, acted, woven, middle, second_held, fetched, ready, left,
    ) = refs
    fetches = [
        pltpu.make_async_copy(second_kernel, second_held, fetched.at[0]),
    ]
    for fetch in fetches:
        fetch.start()
    pitch = cols + EDGE
    depth = CHANNELS
    place = lax.broadcasted_iota(jnp.int32, (EDGE, 1), 0)
    half = 2 * depth
    _, windows, piece, _ = outer.shape
    per = TILE_COLS // piece
    if count > 1:
        each = middle.shape[0] // count
        for k in range(count):
            for j in range(each):
                middle[twist ^ (k * each + j)] = middles[k][j]
    else:
        middle[...] = middles[0][...]

    def side(token, lanes, first):
        within = 0 if first else per - 1
        if token == 0 or token == rows + 1:
            edge, at = side_outer, (0 if token == 0 else rows // 2 + 1)
        else:
            part, at = line_of(token - 1, rows)
            edge, at = (side_middle, at) if part else (side_outer, at + 1)
        at = at * per + within
        if edge is side_middle:
            found = edge[pl.ds(at ^ twist, 1), lanes]
        else:
            found = edge[at : at + 1, lanes]
        return jnp.where(core == (0 if first else 1), found, 0.0)

    def gap_of(row):
        block = jnp.zeros((EDGE, half), jnp.float32)
        if row >= 1:
            token, sub = (row - 1) // 2, (row - 1) % 2
            block = jnp.where(place == 0, side(token, slice(sub * half, (sub + 1) * half), True), block)
        if row < 2 * (rows + 2):
            token, sub = row // 2, row % 2
            block = jnp.where(
                place == EDGE - 1, side(token, slice(sub * half, (sub + 1) * half), False), block
            )
        return block

    taken[0:EDGE, 0:depth] = jnp.zeros((EDGE, depth), jnp.bfloat16)
    for i in range(rows + 2):
        if i == 0:
            source, at = above, 0
        elif i == rows + 1:
            source, at = below, 0
        else:
            part, at = line_of(i - 1, rows)
            source = (outer, middle)[part]
        body = jnp.concatenate(
            [
                source[at * per + across, window].astype(jnp.float32)
                for window in range(windows)
                for across in range(per)
            ],
            axis=0,
        )
        for p in range(2):
            lanes = slice(p * half, (p + 1) * half)
            y = 2 * i + p
            line = jnp.concatenate([gap_of(y), body[:, lanes], gap_of(y + 1)], axis=0)
            length = line.shape[0]
            base = y * pitch
            taken[base : base + length, depth : 3 * depth] = line.astype(jnp.bfloat16)
            later = pltpu.roll(line[:, depth:], 1, 0)
            sooner = pltpu.roll(line[:, :depth], length - 1, 0)
            taken[base + EDGE : base + length, 0:depth] = later[EDGE:].astype(jnp.bfloat16)
            taken[base : base + pitch, 3 * depth :] = sooner[:pitch].astype(jnp.bfloat16)
    last = 2 * (rows + 2) * pitch
    taken[last : last + EDGE, 3 * depth :] = jnp.zeros((EDGE, depth), jnp.bfloat16)

    lines = 2 * rows
    total = (lines + 2) * pitch + EDGE
    even[0:EDGE] = jnp.zeros((EDGE, depth), jnp.float32)
    odd[0:EDGE] = jnp.zeros((EDGE, depth), jnp.float32)
    even[EDGE + total :] = jnp.zeros((EDGE, depth), jnp.float32)
    odd[EDGE + total :] = jnp.zeros((EDGE, depth), jnp.float32)

    def taps(source, kernel, starts, size, q):
        found = None
        for r in range(3):
            cells = [
                source[at + r * pitch : at + r * pitch + size, q * depth : (q + 3) * depth]
                for at in starts
            ]
            cells = cells[0] if len(cells) == 1 else jnp.concatenate(cells, axis=0)
            part = jnp.dot(cells, kernel[r], preferred_element_type=jnp.float32)
            found = part if found is None else found + part
        return found

    step = -(-total // 6 // EDGE) * EDGE
    for at in range(0, total, step):
        size = min(step, total - at)
        kept = keep[at : at + size, :] > 0.0
        kept = jnp.concatenate([kept] * (depth // LANES), axis=1)
        for q, held in ((0, even), (1, odd)):
            value = taps(taken, first_kernel, [at], size, q) + first_bias[...]
            value = jax.nn.gelu(value)
            held[EDGE + at : EDGE + at + size] = jnp.where(kept, value, 0.0)
    acted[:, depth : 2 * depth] = even[EDGE : EDGE + total].astype(jnp.bfloat16)
    acted[:, 2 * depth : 3 * depth] = odd[EDGE : EDGE + total].astype(jnp.bfloat16)
    acted[:, 0:depth] = odd[EDGE - 1 : EDGE - 1 + total].astype(jnp.bfloat16)
    acted[:, 3 * depth :] = even[EDGE + 1 : EDGE + 1 + total].astype(jnp.bfloat16)

    fetches[0].wait()
    group = max(lines // 8, 1)
    leaving = []
    for at in range(0, lines, group):
        for q in range(2):
            starts = [EDGE + (at + y) * pitch for y in range(group)]
            value = taps(acted, second_held, starts, cols, q) + second_bias[...]
            for y in range(group):
                for lane in range(depth // LANES):
                    woven[lane, pl.ds((at + y) * 2 * cols + q, cols, stride=2), :] = value[
                        y * cols : (y + 1) * cols, lane * LANES : (lane + 1) * LANES
                    ]
        rows_here = pl.ds(at * 2 * cols, group * 2 * cols)
        for lane in range(depth // LANES):
            ready[rows_here, lane * LANES : (lane + 1) * LANES] = woven[lane, rows_here, :].astype(
                jnp.bfloat16
            )
        copy = pltpu.make_async_copy(ready.at[rows_here], out.at[rows_here], left.at[at // group])
        copy.start()
        leaving.append(copy)
    for copy in leaving:
        copy.wait()


def convolve_twice(
    scalars, middles, outer, above, below, side_outer, side_middle, keep,
    first_kernel, first_bias, second_kernel, second_bias,
):
    places, windows, piece, width = outer.shape
    rows, cols = 2 * places * piece // TILE_COLS, windows * TILE_COLS
    pitch = cols + EDGE
    total = (2 * rows + 2) * pitch + EDGE
    depth = CHANNELS
    near = pl.BlockSpec(memory_space=pltpu.VMEM)
    far = pl.BlockSpec(memory_space=pltpu.HBM)
    kernels = [kernel.reshape(3, 3 * depth, depth) for kernel in (first_kernel, second_kernel)]
    kernels[1] = pltpu.with_memory_space_constraint(kernels[1], pltpu.HBM)
    found = pl.pallas_call(
        functools.partial(conv_kernel, rows, cols, len(middles)),
        out_shape=pltpu.HBM((4 * rows * cols, depth), jnp.bfloat16),
        in_specs=[pl.BlockSpec(memory_space=pltpu.SMEM)]
        + [near] * (len(middles) + 6)
        + [near, near, far, near],
        out_specs=far,
        scratch_shapes=[
            pltpu.VMEM(((2 * rows + 4) * pitch + EDGE, 4 * depth), jnp.bfloat16),
            pltpu.VMEM((total + 2 * EDGE, depth), jnp.float32),
            pltpu.VMEM((total + 2 * EDGE, depth), jnp.float32),
            pltpu.VMEM((total, 4 * depth), jnp.bfloat16),
            pltpu.VMEM((depth // LANES, 4 * rows * cols, LANES), jnp.float32),
            pltpu.VMEM(outer.shape, jnp.bfloat16),
            pltpu.VMEM((3, 3 * depth, depth), jnp.bfloat16),
            pltpu.SemaphoreType.DMA((1,)),
            pltpu.VMEM((4 * rows * cols, depth), jnp.bfloat16),
            pltpu.SemaphoreType.DMA((2 * rows,)),
        ],
        compiler_params=params(size=2 * VMEM_BYTES),
    )(
        scalars, *middles, outer, above, below, side_outer, side_middle, keep,
        kernels[0], first_bias.reshape(1, depth), kernels[1], second_bias.reshape(1, depth),
    )
    return found.reshape(2 * rows, 2 * cols, depth)


def kept_rows(rows, cols):
    pitch = cols + EDGE
    lines = 2 * rows
    total = (lines + 2) * pitch + EDGE
    row, col = lax.axis_index("row"), lax.axis_index("col")
    top, bottom = row == 0, row == lax.axis_size("row") - 1
    start, end = col == 0, col == lax.axis_size("col") - 1
    flat = jnp.arange(total)
    line, place = flat // pitch - 1, flat % pitch - EDGE
    wrapped = place == -EDGE
    line = jnp.where(wrapped, line - 1, line)
    place = jnp.where(wrapped, cols, place)
    outside = (
        ((line < 0) & top) | ((line >= lines) & bottom)
        | ((place < 0) & start) | ((place >= cols) & end)
    )
    return jnp.broadcast_to(jnp.where(outside, 0.0, 1.0)[:, None], (total, LANES)).astype(jnp.float32)


def shifted(value, axis, by):
    size = lax.axis_size(axis)
    pairs = [(i, i + by) for i in range(size) if 0 <= i + by < size]
    return lax.ppermute(value, axis, pairs)


def swapped(value, axis, by):
    return lax.ppermute(value, axis, [(i, i ^ by) for i in range(lax.axis_size(axis))])


def exchanged(value, axes):
    return lax.all_to_all(value, axes, split_axis=0, concat_axis=0, tiled=True)


def in_pieces(value):
    places, windows, owned, width = value.shape
    if owned < PIECE:
        joined = value.reshape(-1, PIECE // owned, windows, owned, width)
        return jnp.swapaxes(joined, 1, 2).reshape(-1, windows, PIECE, width)
    cut = value.reshape(places, windows, owned // PIECE, PIECE, width)
    return jnp.swapaxes(cut, 1, 2).reshape(-1, windows, PIECE, width)


def picked(value, index, axis=0):
    return lax.dynamic_index_in_dim(value, index, axis, keepdims=False)


def after(value, *earlier):
    corners = tuple(array[(0,) * (array.ndim - 2)][:PIECE, :LANES] for array in earlier)
    return lax.optimization_barrier((value,) + corners)[0]


def shards(
    query_window, key_window, value_window, query_index, key_index,
    proj_weight, proj_bias, first_kernel, first_bias, second_kernel, second_bias,
):
    rows_dev, cols_dev, tokens_win, features = query_window.shape
    windows = rows_dev * cols_dev
    flat = (windows, tokens_win, features)
    inner, cores, places = 2, lax.axis_size("col"), lax.axis_size("row")
    outer = places // inner
    row, core = lax.axis_index("row"), lax.axis_index("col")
    z, y = row // inner, row % inner
    chunk = tokens_win // 2
    owned = chunk // places
    half = features // cores

    def slab_of(value, part, place, count):
        at = place * owned
        if part == 0:
            at = jnp.where(at < chunk // 2, at, at + chunk)
        else:
            at = at + chunk // 2
        cut = lax.dynamic_slice_in_dim(value, at, count * owned, axis=value.ndim - 2)
        return cut.reshape(cut.shape[:-2] + (count, owned, cut.shape[-1]))

    query, key_rows = query_index.reshape(flat), key_index.reshape(flat)
    pair = exchanged(
        dealt(query, key_rows, places, cores).reshape(places * cores, 2, 2, windows * owned, half),
        ("row", "col"),
    ).reshape(places, cores, 2, 2, windows * owned, half)

    window_out = window_attend(
        query_window.reshape(flat), key_window.reshape(flat),
        value_window.reshape(flat), cores,
    )
    window_out = jnp.stack([picked(window_out, core), swapped(picked(window_out, 1 - core), "col", 1)])
    blocks = jnp.stack(
        [
            jnp.stack([slab_of(window_out, part, (z ^ k) * inner, inner) for part in range(2)])
            for k in range(outer)
        ]
    )
    values_near, values_far = picked(blocks, y, 4), swapped(picked(blocks, 1 - y, 4), "row", 1)
    pieces = []
    for part in range(2):
        pieces.append([])
        for k in range(outer):
            piece = jnp.stack([values_near[k, part], values_far[k, part]])
            piece = piece.reshape(inner, cores, windows * owned, half)
            pieces[part].append(swapped(piece, "row", k * inner) if k else piece)
    weights = index_weights(core, pair, owned)
    keep = kept_rows(rows_dev * TILE_ROWS, cols_dev * TILE_COLS)

    images = []
    earlier = []
    line = TILE_COLS // PIECE

    def projected_of(part, apart):
        near, far = index_mix(row, weights[part], pieces[part], part > 0)
        return project(
            near, swapped(far, "col", 1), proj_weight, proj_bias, core, row, places, apart
        )

    projected = gated(projected_of(0, 0)[0], pieces[1])
    outer_rows = in_pieces(exchanged(projected.reshape(places, windows, owned, -1), "row"))
    above = shifted(outer_rows[-line:], "row", 1)
    below = shifted(outer_rows[:line], "row", -1)
    side_outer = swapped(next_column(core, [above, outer_rows, below]), "col", 1)
    if owned == PIECE:
        middles = [
            (swapped(block, "row", k) if k else block).reshape(1, windows, owned, -1)
            for k, block in enumerate(projected_of(1, places))
        ]
        twist = row
    else:
        projected = projected_of(1, 0)[0].reshape(places, windows, owned, -1)
        middles = [in_pieces(exchanged(projected, "row"))]
        twist = jnp.zeros_like(row)
    side_middle = swapped(next_column(core, middles), "col", 1)
    return convolve_twice(
        jnp.stack([core, twist]), middles, outer_rows, above, below, side_outer, side_middle, keep,
        first_kernel, first_bias, second_kernel, second_bias,
    )


def solution(mesh):
    spread = P(("grp", "row"), "col", None, None)
    in_specs = (spread,) * 5 + (P(),) * 6
    out_specs = P(("grp", "row"), "col", None)
    return jax.shard_map(shards, mesh=mesh, in_specs=in_specs, out_specs=out_specs, check_vma=False)
```

```python
import functools
import math

import jax
import jax.numpy as jnp
from jax import lax
from jax.experimental import pallas as pl
from jax.experimental.pallas import tpu as pltpu
from jax.sharding import PartitionSpec as P

HEADS = 8
HEAD_DIM = 160
CHANNELS = 256
TILE_ROWS = 8
TILE_COLS = 16
LANES = 128
EDGE = 16
PIECE = 8
SPAN = 2 * LANES
VMEM_BYTES = 12 * 1024 * 1024


def params(steps=0, size=VMEM_BYTES):
    return pltpu.CompilerParams(
        dimension_semantics=("arbitrary",) * steps if steps else None,
        vmem_limit_bytes=size,
    )


def head_start(head):
    return head * HEAD_DIM // LANES * LANES


def head_mask(head):
    lane = lax.broadcasted_iota(jnp.int32, (1, SPAN), 1) + head_start(head)
    return (lane >= head * HEAD_DIM) & (lane < (head + 1) * HEAD_DIM)


def joined_heads(mixed):
    tiles = []
    lane = lax.broadcasted_iota(jnp.int32, (1, LANES), 1)
    for tile in range(len(mixed) * HEAD_DIM // LANES):
        base = tile * LANES
        first, last = base // HEAD_DIM, (base + LANES - 1) // HEAD_DIM
        pieces = []
        for head in (first, last):
            at = base - head_start(head)
            pieces.append(mixed[head][:, at : at + LANES])
        if first == last:
            tiles.append(pieces[0])
        else:
            tiles.append(jnp.where(lane < last * HEAD_DIM - base, pieces[0], pieces[1]))
    return jnp.concatenate(tiles, axis=1)


def softmax_rows(scores):
    raised = jnp.exp(scores - jnp.max(scores, axis=-1, keepdims=True))
    return (raised / jnp.sum(raised, axis=-1, keepdims=True)).astype(jnp.bfloat16)


def window_kernel(query, key_rows, value, out):
    mixed = []
    for head in range(HEADS):
        lanes = pl.ds(head_start(head), SPAN)
        masked = jnp.where(head_mask(head), query[0, :, lanes], 0)
        scores = lax.dot_general(
            masked, key_rows[0, :, lanes], (((1,), (1,)), ((), ())),
            preferred_element_type=jnp.float32,
        ) * (1.0 / math.sqrt(HEAD_DIM))
        mixed.append(
            jnp.dot(softmax_rows(scores), value[0, :, lanes], preferred_element_type=jnp.float32)
        )
    joined = joined_heads(mixed).astype(jnp.bfloat16)
    parts, features = out.shape[0], out.shape[-1]
    for part in range(parts):
        out[part, 0] = joined[:, part * features : (part + 1) * features]


def window_attend(query, key_rows, value, parts):
    windows, tokens, features = query.shape
    result = (parts, windows, tokens, features // parts)
    block = pl.BlockSpec((1, tokens, features), lambda w: (w, 0, 0))
    return pl.pallas_call(
        window_kernel,
        grid=(windows,),
        in_specs=[block] * 3,
        out_specs=pl.BlockSpec((parts, 1, tokens, features // parts), lambda w: (0, w, 0, 0)),
        out_shape=jax.ShapeDtypeStruct(result, jnp.bfloat16),
        compiler_params=params(1),
    )(query, key_rows, value)


def token_of(place, part, owned, places):
    chunk = owned * places
    if part:
        return chunk // 2 + place * owned
    return place * owned if place * owned < chunk // 2 else chunk + place * owned


def deal_kernel(query, key_rows, out, held, packed, arrived, left):
    places, cores, parts, kinds, block, half = out.shape
    windows = query.shape[0]
    owned = block // windows
    arriving = [
        pltpu.make_async_copy(source, held.at[kind], arrived.at[kind])
        for kind, source in enumerate((query, key_rows))
    ]
    for copy in arriving:
        copy.start()
    leaving = []
    for kind in range(kinds):
        arriving[kind].wait()
        for place in range(places):
            for part in range(parts):
                rows = pl.ds(token_of(place, part, owned, places), owned)
                for window in range(windows):
                    for core in range(cores):
                        packed[kind, place, core, part, pl.ds(window * owned, owned), :] = held[
                            kind, window, rows, core * half : (core + 1) * half
                        ]
        copy = pltpu.make_async_copy(packed.at[kind], out.at[:, :, :, kind], left.at[kind])
        copy.start()
        leaving.append(copy)
    for copy in leaving:
        copy.wait()


def dealt(query, key_rows, places, cores):
    windows, tokens, features = query.shape
    result = (places, cores, 2, 2, windows * tokens // (2 * places), features // cores)
    return pl.pallas_call(
        deal_kernel,
        in_specs=[pl.BlockSpec(memory_space=pltpu.HBM)] * 2,
        out_specs=pl.BlockSpec(memory_space=pltpu.HBM),
        out_shape=pltpu.HBM(result, query.dtype),
        scratch_shapes=[
            pltpu.VMEM((2,) + query.shape, query.dtype),
            pltpu.VMEM((2,) + result[:3] + result[4:], query.dtype),
            pltpu.SemaphoreType.DMA((2,)),
            pltpu.SemaphoreType.DMA((2,)),
        ],
        compiler_params=params(),
    )(
        pltpu.with_memory_space_constraint(query, pltpu.HBM),
        pltpu.with_memory_space_constraint(key_rows, pltpu.HBM),
    )


def weights_kernel(tokens, core, pair, *outs):
    places, cores, _, _, block, _ = pair.shape
    head = pl.program_id(1)
    start = head * HEAD_DIM // LANES * LANES
    lanes = pl.ds(pl.multiple_of(start, LANES), SPAN)
    lane = lax.broadcasted_iota(jnp.int32, (1, SPAN), 1) + start
    inside = (lane >= head * HEAD_DIM) & (lane < (head + 1) * HEAD_DIM)
    held = jnp.float32 if block % EDGE else jnp.bfloat16

    def gathered(kind):
        return jnp.concatenate(
            [
                pair[place, core[0] ^ far, 0, kind, :, lanes].astype(held)
                for far in range(cores)
                for place in range(places)
            ],
            axis=0,
        ).astype(jnp.bfloat16)

    scores = lax.dot_general(
        jnp.where(inside, gathered(0), 0), gathered(1), (((1,), (1,)), ((), ())),
        preferred_element_type=jnp.float32,
    ) * (1.0 / math.sqrt(HEAD_DIM))
    rows = scores.shape[0]
    token_row = lax.broadcasted_iota(jnp.int32, (rows, 1), 0) % tokens
    token_col = lax.broadcasted_iota(jnp.int32, (1, rows), 1) % tokens
    found = softmax_rows(jnp.where(token_row == token_col, scores, -jnp.inf))
    for part, out in enumerate(outs):

        @pl.when(pl.program_id(0) == part)
        def _(out=out):
            out[0] = found


def index_weights(core, pair, tokens):
    places, cores, parts, kinds, block, features = pair.shape
    heads = features // HEAD_DIM
    rows = places * cores * block
    return pl.pallas_call(
        functools.partial(weights_kernel, tokens),
        grid=(parts, heads),
        in_specs=[
            pl.BlockSpec(memory_space=pltpu.SMEM),
            pl.BlockSpec((places, cores, 1, kinds, block, features), lambda p, h: (0, 0, p, 0, 0, 0)),
        ],
        out_specs=[
            pl.BlockSpec(
                (1, rows, rows),
                lambda p, h, part=part: (jnp.where(p < part, 0, jnp.where(p == part, h, heads - 1)), 0, 0),
            )
            for part in range(parts)
        ],
        out_shape=[
            pltpu.VMEM((heads, rows, rows), jnp.bfloat16) for part in range(parts)
        ],
        compiler_params=params(2),
    )(core.reshape(1), pair)


def mix_kernel(fetched, place, weights, *refs):
    pieces, (near, far, value, held, arrived) = refs[:-5], refs[-5:]
    each, cores, rows, features = pieces[0].shape
    half = value.shape[0] // cores
    heads = features // HEAD_DIM
    copies = []
    if fetched:
        copies = [
            pltpu.make_async_copy(piece, held.at[k], arrived.at[k]) for k, piece in enumerate(pieces)
        ]
    for copy in copies:
        copy.start()
    for k, piece in enumerate(pieces):
        if fetched:
            copies[k].wait()
            piece = held.at[k]
        for j in range(each):
            at = pl.multiple_of((place[0] ^ (k * each + j)) * rows, rows)
            for core in range(cores):
                value[pl.ds(core * half + at, rows), :] = piece[j, core].astype(value.dtype)
    mixed = []
    for head in range(heads):
        lanes = slice(head_start(head), head_start(head) + SPAN)
        mixed.append(
            jnp.dot(
                weights[head], value[:, lanes].astype(jnp.bfloat16),
                preferred_element_type=jnp.float32,
            )
        )
    joined = joined_heads(mixed).astype(jnp.bfloat16)
    near[...] = joined[:half]
    far[...] = joined[half:]


def index_mix(place, weights, pieces, fetched):
    heads, rows, _ = weights.shape
    features = pieces[0].shape[-1]
    result = pltpu.VMEM((rows // 2, features), jnp.bfloat16)
    held = jnp.float32 if pieces[0].shape[2] % EDGE else jnp.bfloat16
    source = pl.BlockSpec(memory_space=pltpu.HBM if fetched else pltpu.VMEM)
    if fetched:
        pieces = [pltpu.with_memory_space_constraint(piece, pltpu.HBM) for piece in pieces]
    return pl.pallas_call(
        functools.partial(mix_kernel, fetched),
        in_specs=[pl.BlockSpec(memory_space=pltpu.SMEM), pl.BlockSpec(memory_space=pltpu.VMEM)]
        + [source] * len(pieces),
        out_specs=[pl.BlockSpec(memory_space=pltpu.VMEM)] * 2,
        out_shape=[result, result],
        scratch_shapes=[
            pltpu.VMEM((rows, features), held),
            pltpu.VMEM((len(pieces),) + pieces[0].shape, jnp.bfloat16),
            pltpu.SemaphoreType.DMA((len(pieces),)),
        ],
        compiler_params=params(),
    )(
        place.reshape(1), weights, *pieces,
    )


def project_kernel(places, inner, scalars, near, far, proj_weight, proj_bias, *refs):
    core, twist = scalars[0], scalars[1]
    half = near.shape[1]
    total = proj_bias[...]
    for held, place in ((near, core), (far, 1 - core)):
        rows = pl.ds(pl.multiple_of(place * half, half), half)
        total = total + jnp.dot(held[...], proj_weight[rows, :], preferred_element_type=jnp.float32)
    total = total.astype(jnp.bfloat16)
    if len(refs) == 1:
        refs[0][...] = total
        return
    *outs, turned = refs
    block = total.shape[0] // places
    for place in range(places):
        turned[place] = total[place * block : (place + 1) * block]
    for k in range(places):
        outs[k % inner][k // inner] = turned[twist ^ k]


def project(near, far, proj_weight, proj_bias, core, row, places, inner):
    rows, width = near.shape[0], proj_weight.shape[1]
    block = rows // places
    shapes = [pltpu.HBM((rows, width), jnp.bfloat16)]
    if inner:
        shapes = [jax.ShapeDtypeStruct((places // inner, block, width), jnp.bfloat16)] * inner
    return pl.pallas_call(
        functools.partial(project_kernel, places, inner),
        in_specs=[pl.BlockSpec(memory_space=pltpu.SMEM)]
        + [pl.BlockSpec(memory_space=pltpu.VMEM)] * 4,
        out_specs=[pl.BlockSpec(memory_space=pltpu.VMEM)] * len(shapes),
        out_shape=shapes,
        scratch_shapes=[pltpu.VMEM((places, block, width), jnp.bfloat16)] if inner else [],
        compiler_params=params(),
    )(jnp.stack([core, row]), near, far, proj_weight, proj_bias.reshape(1, -1))


def gate_kernel(*refs):
    del refs


def gated(value, earlier):
    anywhere = pl.BlockSpec(memory_space=pl.ANY)
    return pl.pallas_call(
        gate_kernel,
        in_specs=[anywhere] * (1 + len(earlier)),
        out_specs=anywhere,
        out_shape=pltpu.HBM(value.shape, value.dtype),
        input_output_aliases={0: 0},
    )(value, *earlier)


def column_kernel(core, *refs):
    *lines, out = refs
    at = 0
    for ref in lines:
        for place in range(ref.shape[0]):
            first = ref[place, 0].astype(jnp.float32)[:1]
            last = ref[place, ref.shape[1] - 1].astype(jnp.float32)[ref.shape[2] - 1 :]
            out[at : at + 1, :] = jnp.where(core[0] == 0, last, first)
            at += 1


def next_column(core, lines):
    total = sum(value.shape[0] for value in lines)
    return pl.pallas_call(
        column_kernel,
        in_specs=[pl.BlockSpec(memory_space=pltpu.SMEM)]
        + [pl.BlockSpec(memory_space=pltpu.VMEM)] * len(lines),
        out_specs=pl.BlockSpec(memory_space=pltpu.VMEM),
        out_shape=jax.ShapeDtypeStruct((total, lines[0].shape[-1]), jnp.float32),
        compiler_params=params(),
    )(core.reshape(1), *lines)


def line_of(line, rows):
    quarter = rows // 4
    if line < quarter:
        return 0, line
    if line < 3 * quarter:
        return 1, line - quarter
    return 0, line - 2 * quarter


def conv_kernel(
    rows, cols, count, scalars, *refs,
):
    core, twist = scalars[0], scalars[1]
    middles, refs = refs[:count], refs[count:]
    (
        outer, above, below, side_outer, side_middle, keep,
        first_kernel, first_bias, second_kernel, second_bias, out,
        taken, even, odd, acted, woven, middle, second_held, fetched, ready, left,
    ) = refs
    fetches = [
        pltpu.make_async_copy(second_kernel, second_held, fetched.at[0]),
    ]
    for fetch in fetches:
        fetch.start()
    pitch = cols + EDGE
    depth = CHANNELS
    place = lax.broadcasted_iota(jnp.int32, (EDGE, 1), 0)
    half = 2 * depth
    _, windows, piece, _ = outer.shape
    per = TILE_COLS // piece
    if count > 1:
        each = middle.shape[0] // count
        for k in range(count):
            for j in range(each):
                middle[twist ^ (k * each + j)] = middles[k][j]
    else:
        middle[...] = middles[0][...]

    def side(token, lanes, first):
        within = 0 if first else per - 1
        if token == 0 or token == rows + 1:
            edge, at = side_outer, (0 if token == 0 else rows // 2 + 1)
        else:
            part, at = line_of(token - 1, rows)
            edge, at = (side_middle, at) if part else (side_outer, at + 1)
        at = at * per + within
        if edge is side_middle:
            found = edge[pl.ds(at ^ twist, 1), lanes]
        else:
            found = edge[at : at + 1, lanes]
        return jnp.where(core == (0 if first else 1), found, 0.0)

    def gap_of(row):
        block = jnp.zeros((EDGE, half), jnp.float32)
        if row >= 1:
            token, sub = (row - 1) // 2, (row - 1) % 2
            block = jnp.where(place == 0, side(token, slice(sub * half, (sub + 1) * half), True), block)
        if row < 2 * (rows + 2):
            token, sub = row // 2, row % 2
            block = jnp.where(
                place == EDGE - 1, side(token, slice(sub * half, (sub + 1) * half), False), block
            )
        return block

    taken[0:EDGE, 0:depth] = jnp.zeros((EDGE, depth), jnp.bfloat16)
    for i in range(rows + 2):
        if i == 0:
            source, at = above, 0
        elif i == rows + 1:
            source, at = below, 0
        else:
            part, at = line_of(i - 1, rows)
            source = (outer, middle)[part]
        body = jnp.concatenate(
            [
                source[at * per + across, window].astype(jnp.float32)
                for window in range(windows)
                for across in range(per)
            ],
            axis=0,
        )
        for p in range(2):
            lanes = slice(p * half, (p + 1) * half)
            y = 2 * i + p
            line = jnp.concatenate([gap_of(y), body[:, lanes], gap_of(y + 1)], axis=0)
            length = line.shape[0]
            base = y * pitch
            taken[base : base + length, depth : 3 * depth] = line.astype(jnp.bfloat16)
            later = pltpu.roll(line[:, depth:], 1, 0)
            sooner = pltpu.roll(line[:, :depth], length - 1, 0)
            taken[base + EDGE : base + length, 0:depth] = later[EDGE:].astype(jnp.bfloat16)
            taken[base : base + pitch, 3 * depth :] = sooner[:pitch].astype(jnp.bfloat16)
    last = 2 * (rows + 2) * pitch
    taken[last : last + EDGE, 3 * depth :] = jnp.zeros((EDGE, depth), jnp.bfloat16)

    lines = 2 * rows
    total = (lines + 2) * pitch + EDGE
    even[0:EDGE] = jnp.zeros((EDGE, depth), jnp.float32)
    odd[0:EDGE] = jnp.zeros((EDGE, depth), jnp.float32)
    even[EDGE + total :] = jnp.zeros((EDGE, depth), jnp.float32)
    odd[EDGE + total :] = jnp.zeros((EDGE, depth), jnp.float32)

    def taps(source, kernel, starts, size, q):
        found = None
        for r in range(3):
            cells = [
                source[at + r * pitch : at + r * pitch + size, q * depth : (q + 3) * depth]
                for at in starts
            ]
            cells = cells[0] if len(cells) == 1 else jnp.concatenate(cells, axis=0)
            part = jnp.dot(cells, kernel[r], preferred_element_type=jnp.float32)
            found = part if found is None else found + part
        return found

    step = -(-total // 6 // EDGE) * EDGE
    for at in range(0, total, step):
        size = min(step, total - at)
        kept = keep[at : at + size, :] > 0.0
        kept = jnp.concatenate([kept] * (depth // LANES), axis=1)
        for q, held in ((0, even), (1, odd)):
            value = taps(taken, first_kernel, [at], size, q) + first_bias[...]
            value = jax.nn.gelu(value)
            held[EDGE + at : EDGE + at + size] = jnp.where(kept, value, 0.0)
    acted[:, depth : 2 * depth] = even[EDGE : EDGE + total].astype(jnp.bfloat16)
    acted[:, 2 * depth : 3 * depth] = odd[EDGE : EDGE + total].astype(jnp.bfloat16)
    acted[:, 0:depth] = odd[EDGE - 1 : EDGE - 1 + total].astype(jnp.bfloat16)
    acted[:, 3 * depth :] = even[EDGE + 1 : EDGE + 1 + total].astype(jnp.bfloat16)

    fetches[0].wait()
    group = max(lines // 8, 1)
    leaving = []
    for at in range(0, lines, group):
        for q in range(2):
            starts = [EDGE + (at + y) * pitch for y in range(group)]
            value = taps(acted, second_held, starts, cols, q) + second_bias[...]
            for y in range(group):
                for lane in range(depth // LANES):
                    woven[lane, pl.ds((at + y) * 2 * cols + q, cols, stride=2), :] = value[
                        y * cols : (y + 1) * cols, lane * LANES : (lane + 1) * LANES
                    ]
        rows_here = pl.ds(at * 2 * cols, group * 2 * cols)
        for lane in range(depth // LANES):
            ready[rows_here, lane * LANES : (lane + 1) * LANES] = woven[lane, rows_here, :].astype(
                jnp.bfloat16
            )
        copy = pltpu.make_async_copy(ready.at[rows_here], out.at[rows_here], left.at[at // group])
        copy.start()
        leaving.append(copy)
    for copy in leaving:
        copy.wait()


def convolve_twice(
    scalars, middles, outer, above, below, side_outer, side_middle, keep,
    first_kernel, first_bias, second_kernel, second_bias,
):
    places, windows, piece, width = outer.shape
    rows, cols = 2 * places * piece // TILE_COLS, windows * TILE_COLS
    pitch = cols + EDGE
    total = (2 * rows + 2) * pitch + EDGE
    depth = CHANNELS
    near = pl.BlockSpec(memory_space=pltpu.VMEM)
    far = pl.BlockSpec(memory_space=pltpu.HBM)
    kernels = [kernel.reshape(3, 3 * depth, depth) for kernel in (first_kernel, second_kernel)]
    kernels[1] = pltpu.with_memory_space_constraint(kernels[1], pltpu.HBM)
    found = pl.pallas_call(
        functools.partial(conv_kernel, rows, cols, len(middles)),
        out_shape=pltpu.HBM((4 * rows * cols, depth), jnp.bfloat16),
        in_specs=[pl.BlockSpec(memory_space=pltpu.SMEM)]
        + [near] * (len(middles) + 6)
        + [near, near, far, near],
        out_specs=far,
        scratch_shapes=[
            pltpu.VMEM(((2 * rows + 4) * pitch + EDGE, 4 * depth), jnp.bfloat16),
            pltpu.VMEM((total + 2 * EDGE, depth), jnp.float32),
            pltpu.VMEM((total + 2 * EDGE, depth), jnp.float32),
            pltpu.VMEM((total, 4 * depth), jnp.bfloat16),
            pltpu.VMEM((depth // LANES, 4 * rows * cols, LANES), jnp.float32),
            pltpu.VMEM(outer.shape, jnp.bfloat16),
            pltpu.VMEM((3, 3 * depth, depth), jnp.bfloat16),
            pltpu.SemaphoreType.DMA((1,)),
            pltpu.VMEM((4 * rows * cols, depth), jnp.bfloat16),
            pltpu.SemaphoreType.DMA((2 * rows,)),
        ],
        compiler_params=params(size=2 * VMEM_BYTES),
    )(
        scalars, *middles, outer, above, below, side_outer, side_middle, keep,
        kernels[0], first_bias.reshape(1, depth), kernels[1], second_bias.reshape(1, depth),
    )
    return found.reshape(2 * rows, 2 * cols, depth)


def kept_rows(rows, cols):
    pitch = cols + EDGE
    lines = 2 * rows
    total = (lines + 2) * pitch + EDGE
    row, col = lax.axis_index("row"), lax.axis_index("col")
    top, bottom = row == 0, row == lax.axis_size("row") - 1
    start, end = col == 0, col == lax.axis_size("col") - 1
    flat = jnp.arange(total)
    line, place = flat // pitch - 1, flat % pitch - EDGE
    wrapped = place == -EDGE
    line = jnp.where(wrapped, line - 1, line)
    place = jnp.where(wrapped, cols, place)
    outside = (
        ((line < 0) & top) | ((line >= lines) & bottom)
        | ((place < 0) & start) | ((place >= cols) & end)
    )
    return jnp.broadcast_to(jnp.where(outside, 0.0, 1.0)[:, None], (total, LANES)).astype(jnp.float32)


def shifted(value, axis, by):
    size = lax.axis_size(axis)
    pairs = [(i, i + by) for i in range(size) if 0 <= i + by < size]
    return lax.ppermute(value, axis, pairs)


def swapped(value, axis, by):
    return lax.ppermute(value, axis, [(i, i ^ by) for i in range(lax.axis_size(axis))])


def exchanged(value, axes):
    return lax.all_to_all(value, axes, split_axis=0, concat_axis=0, tiled=True)


def in_pieces(value):
    places, windows, owned, width = value.shape
    if owned < PIECE:
        joined = value.reshape(-1, PIECE // owned, windows, owned, width)
        return jnp.swapaxes(joined, 1, 2).reshape(-1, windows, PIECE, width)
    cut = value.reshape(places, windows, owned // PIECE, PIECE, width)
    return jnp.swapaxes(cut, 1, 2).reshape(-1, windows, PIECE, width)


def picked(value, index, axis=0):
    return lax.dynamic_index_in_dim(value, index, axis, keepdims=False)


def after(value, *earlier):
    corners = tuple(array[(0,) * (array.ndim - 2)][:PIECE, :LANES] for array in earlier)
    return lax.optimization_barrier((value,) + corners)[0]


def shards(
    query_window, key_window, value_window, query_index, key_index,
    proj_weight, proj_bias, first_kernel, first_bias, second_kernel, second_bias,
):
    rows_dev, cols_dev, tokens_win, features = query_window.shape
    windows = rows_dev * cols_dev
    flat = (windows, tokens_win, features)
    inner, cores, places = 2, lax.axis_size("col"), lax.axis_size("row")
    outer = places // inner
    row, core = lax.axis_index("row"), lax.axis_index("col")
    z, y = row // inner, row % inner
    chunk = tokens_win // 2
    owned = chunk // places
    half = features // cores

    def slab_of(value, part, place, count):
        at = place * owned
        if part == 0:
            at = jnp.where(at < chunk // 2, at, at + chunk)
        else:
            at = at + chunk // 2
        cut = lax.dynamic_slice_in_dim(value, at, count * owned, axis=value.ndim - 2)
        return cut.reshape(cut.shape[:-2] + (count, owned, cut.shape[-1]))

    query, key_rows = query_index.reshape(flat), key_index.reshape(flat)
    pair = exchanged(
        dealt(query, key_rows, places, cores).reshape(places * cores, 2, 2, windows * owned, half),
        ("row", "col"),
    ).reshape(places, cores, 2, 2, windows * owned, half)

    window_out = window_attend(
        query_window.reshape(flat), key_window.reshape(flat),
        value_window.reshape(flat), cores,
    )
    window_out = jnp.stack([picked(window_out, core), swapped(picked(window_out, 1 - core), "col", 1)])
    blocks = jnp.stack(
        [
            jnp.stack([slab_of(window_out, part, (z ^ k) * inner, inner) for part in range(2)])
            for k in range(outer)
        ]
    )
    values_near, values_far = picked(blocks, y, 4), swapped(picked(blocks, 1 - y, 4), "row", 1)
    pieces = []
    for part in range(2):
        pieces.append([])
        for k in range(outer):
            piece = jnp.stack([values_near[k, part], values_far[k, part]])
            piece = piece.reshape(inner, cores, windows * owned, half)
            pieces[part].append(swapped(piece, "row", k * inner) if k else piece)
    weights = index_weights(core, pair, owned)
    keep = kept_rows(rows_dev * TILE_ROWS, cols_dev * TILE_COLS)

    images = []
    earlier = []
    line = TILE_COLS // PIECE

    def projected_of(part, apart):
        near, far = index_mix(row, weights[part], pieces[part], part > 0)
        return project(
            near, swapped(far, "col", 1), proj_weight, proj_bias, core, row, places, apart
        )

    projected = gated(projected_of(0, 0)[0], pieces[1])
    outer_rows = in_pieces(exchanged(projected.reshape(places, windows, owned, -1), "row"))
    above = shifted(outer_rows[-line:], "row", 1)
    below = shifted(outer_rows[:line], "row", -1)
    side_outer = swapped(next_column(core, [above, outer_rows, below]), "col", 1)
    if owned == PIECE:
        middles = [
            (swapped(block, "row", k) if k else block).reshape(1, windows, owned, -1)
            for k, block in enumerate(projected_of(1, places))
        ]
        twist = row
    else:
        projected = projected_of(1, 0)[0].reshape(places, windows, owned, -1)
        middles = [in_pieces(exchanged(projected, "row"))]
        twist = jnp.zeros_like(row)
    side_middle = swapped(next_column(core, middles), "col", 1)
    return convolve_twice(
        jnp.stack([core, twist]), middles, outer_rows, above, below, side_outer, side_middle, keep,
        first_kernel, first_bias, second_kernel, second_bias,
    )


def solution(mesh):
    spread = P(("grp", "row"), "col", None, None)
    in_specs = (spread,) * 5 + (P(),) * 6
    out_specs = P(("grp", "row"), "col", None)
    return jax.shard_map(shards, mesh=mesh, in_specs=in_specs, out_specs=out_specs, check_vma=False)
```
